256 devices in a mesh: win: 8 (over x, y_hi), col: 32 (over y_lo, z, core).
Axes of the slice: x: 4, y: 4 (y_hi: 2, y_lo: 2; y = y_hi * 2 + y_lo), z: 8, core: 2. Of those that a mesh axis runs over, the one named last changes fastest.
Arguments:
- increment: float32 [8, 32768, 128], P('win', 'col'), may hold values from -6 to 6
- dual_field: float32 [8, 32768, 128], P('win', 'col'), may hold values from -6 to 6
- departure: float32 [8, 32768, 128], P('win', 'col'), may hold values from -6 to 6
- obs_grad: float32 [8, 32768, 128], P('win', 'col'), may hold values from -6 to 6
- obs_weight: bfloat16 [8, 32768, 128], P('win', 'col'), may hold values from 0.099609375 to 4
- error_scale: float32 [8, 128], P('win'), may hold values from 0.4 to 1.6
- corr_blocks: bfloat16 [512, 64, 512], P('col')
- corr_pattern: int32 [512, 8], P('col'), may hold values from 0 to 511, as said below
- model_blocks: bfloat16 [512, 64, 256], P('col')
- model_pattern: int32 [512, 4], P('col'), may hold values from 0 to 511, as said below
Outputs:
- increment_next: float32 [8, 32768, 128], P('win', 'col')
- dual_next: float32 [8, 32768, 128], P('win', 'col')
The draws below stay inside these ranges and needn't reach their ends.
Inputs may be any that keep to these rules, and one draw needn't show every extreme that they name: `corr_pattern`: each row i names distinct block columns within 4 blocks of i around the cycle of 512 blocks; slot 0 names i itself. `model_pattern`: each row i names distinct block columns within 2 blocks of i around the cycle of 512 blocks; slot 0 names i itself.
All inputs are finite; a program needn't handle non-finite values.
Results may differ from the reference program's by a relative error of at most 0.0046.
Values may be sent and summed in bfloat16 or wider, within the bound.
A program may use at most 64 MiB of HBM per device.

```python
import math
import jax
import jax.numpy as jnp
from jax import lax

LEV = 128
BLK = 64
RU = 4
NNZ_U = 8
RM = 2
NNZ_M = 4
SUB = 8
NB = 512
COLS = 32768


def band_pattern(key, reach_blocks, slot_count):
    row_index = jnp.arange(NB, dtype=jnp.int32)
    offer_count = 2 * reach_blocks
    scores = jax.random.randint(key, (NB, offer_count), 0, 1 << 20) * offer_count + jnp.arange(offer_count, dtype=jnp.int32)[None, :]
    ranking = jnp.argsort(scores, axis=1)
    candidates = jnp.concatenate([jnp.arange(-reach_blocks, 0, dtype=jnp.int32), jnp.arange(1, reach_blocks + 1, dtype=jnp.int32)])
    chosen = candidates[ranking[:, :slot_count - 1]]
    offsets = jnp.concatenate([jnp.zeros((NB, 1), jnp.int32), chosen], axis=1)
    return ((row_index[:, None] + offsets) % NB).astype(jnp.int32)


def unit_part(slot_count):
    row_index = jnp.arange(BLK)[:, None]
    column_index = jnp.arange(slot_count * BLK)[None, :]
    return (row_index == column_index).astype(jnp.float32)


def draw_corr_pattern(key, part):
    key = jax.random.fold_in(key, 11)
    return band_pattern(key, RU, NNZ_U)


def draw_model_pattern(key, part):
    key = jax.random.fold_in(key, 12)
    return band_pattern(key, RM, NNZ_M)


def draw_corr_blocks(key, part):
    key = jax.random.fold_in(key, 13)
    spread = 1.5 / (NNZ_U * BLK) ** 0.5
    shape = (NB, BLK, NNZ_U * BLK)
    values = jax.random.uniform(key, shape, jnp.float32, -1.0, 1.0)
    unit = unit_part(NNZ_U)[None]
    return (spread * values * (1.0 - unit) + unit).astype(jnp.bfloat16)


def draw_model_blocks(key, part):
    key = jax.random.fold_in(key, 14)
    spread = 0.45 / (NNZ_M * BLK) ** 0.5
    shape = (NB, BLK, NNZ_M * BLK)
    values = jax.random.uniform(key, shape, jnp.float32, -1.0, 1.0)
    unit = unit_part(NNZ_M)[None]
    return (spread * values * (1.0 - unit) + 0.5 * unit).astype(jnp.bfloat16)


def shard_levels(rng, shape, pieces, least, largest):
    level, own = 1.0, jax.random.fold_in(rng, 6)
    for axis_at, blocks in pieces:
        draws = jnp.exp(jax.random.uniform(jax.random.fold_in(own, axis_at), (blocks,), jnp.float32, least / len(pieces), largest / len(pieces)))
        level = level * jnp.repeat(draws, shape[axis_at] // blocks).reshape([-1 if axis == axis_at else 1 for axis in range(len(shape))])
    return level


def noise(own_key, dims, width, reach, shards=(), held_as=jnp.bfloat16):
    drawn = width * jax.random.normal(own_key, dims, jnp.float32)
    if shards:
        drawn = drawn * shard_levels(own_key, dims, shards, -0.22, 0.18)
    return jnp.clip(drawn, -reach, reach).astype(held_as)


def setup_inputs(seed: int = 0) -> dict:
    key_list = jax.random.split(jax.random.key(seed), 11)
    increment = noise(key_list[0], (SUB, COLS, LEV), 1.0, 6.0, ((0, 8), (1, 32)), jnp.float32)
    dual_field = noise(key_list[1], (SUB, COLS, LEV), 1.0, 6.0, ((0, 8), (1, 32)), jnp.float32)
    departure = noise(key_list[2], (SUB, COLS, LEV), 1.0, 6.0, ((0, 8), (1, 32)), jnp.float32)
    obs_grad = noise(key_list[3], (SUB, COLS, LEV), 1.0, 6.0, ((0, 8), (1, 32)), jnp.float32)
    obs_weight = jnp.clip(jnp.exp(math.log(4.0) - 3.6927934 * jax.random.uniform(key_list[4], (SUB, COLS, LEV), jnp.float32) ** shard_levels(key_list[4], (SUB, COLS, LEV), ((0, 8), (1, 32)), -0.2, 0.2)), 0.099609375, 4.0).astype(jnp.bfloat16)
    error_scale = jnp.clip(jnp.exp(math.log(1.6) - 1.3862944 * jax.random.uniform(key_list[5], (SUB, LEV), jnp.float32) ** shard_levels(key_list[5], (SUB, LEV), ((0, 8),), -0.2, 0.2)), 0.4, 1.6)
    corr_blocks = draw_corr_blocks(jax.random.fold_in(key_list[10], 71), 0)
    corr_pattern = draw_corr_pattern(jax.random.fold_in(key_list[10], 71), 0)
    model_blocks = draw_model_blocks(jax.random.fold_in(key_list[10], 71), 0)
    model_pattern = draw_model_pattern(jax.random.fold_in(key_list[10], 71), 0)
    return dict(increment=increment, dual_field=dual_field, departure=departure, obs_grad=obs_grad, obs_weight=obs_weight, error_scale=error_scale, corr_blocks=corr_blocks, corr_pattern=corr_pattern, model_blocks=model_blocks, model_pattern=model_pattern)


relax_factor = 0.75


def forward_apply(blocks, pattern, field):
    field_blocks = field.astype(jnp.float32).reshape(NB, BLK, LEV)
    totals = jnp.zeros((NB, BLK, LEV), jnp.float32)
    for slot_index in range(pattern.shape[1]):
        block_part = blocks[:, :, slot_index * BLK:(slot_index + 1) * BLK].astype(jnp.float32)
        totals = totals + jnp.einsum("iac,icl->ial", block_part, field_blocks[pattern[:, slot_index]], precision=lax.Precision.HIGHEST)
    return totals.reshape(COLS, LEV)


def adjoint_apply(blocks, pattern, field):
    field_blocks = field.astype(jnp.float32).reshape(NB, BLK, LEV)
    totals = jnp.zeros((NB, BLK, LEV), jnp.float32)
    for slot_index in range(pattern.shape[1]):
        block_part = blocks[:, :, slot_index * BLK:(slot_index + 1) * BLK].astype(jnp.float32)
        contrib = jnp.einsum("iac,ial->icl", block_part, field_blocks, precision=lax.Precision.HIGHEST)
        totals = totals.at[pattern[:, slot_index]].add(contrib)
    return totals.reshape(COLS, LEV)


def reference(increment, dual_field, departure, obs_grad, obs_weight, error_scale, corr_blocks, corr_pattern, model_blocks, model_pattern):
    scaling = error_scale[:, None, :]

    def forward_all(blocks, pattern, field):
        return lax.map(lambda vector: forward_apply(blocks, pattern, vector), field)

    def adjoint_all(blocks, pattern, field):
        return lax.map(lambda vector: adjoint_apply(blocks, pattern, vector), field)

    def covariance(field):
        scaled = (scaling * field).astype(jnp.bfloat16)
        inner_term = adjoint_all(corr_blocks, corr_pattern, scaled).astype(jnp.bfloat16)
        return scaling * forward_all(corr_blocks, corr_pattern, inner_term)

    advanced = forward_all(model_blocks, model_pattern, increment.astype(jnp.bfloat16))
    before = jnp.concatenate([jnp.zeros_like(advanced[:1]), advanced[:-1]], axis=0)
    resid_dual = departure - covariance(dual_field) - (increment - before)
    pulled = adjoint_all(model_blocks, model_pattern, dual_field.astype(jnp.bfloat16))
    after_terms = jnp.concatenate([pulled[1:], jnp.zeros_like(pulled[:1])], axis=0)
    resid_incr = obs_weight.astype(jnp.float32) * increment - obs_grad - (dual_field - after_terms)

    def back_step(running, resid):
        running = resid + adjoint_apply(model_blocks, model_pattern, running.astype(jnp.bfloat16))
        return running, running

    initial = jnp.zeros((COLS, LEV), jnp.float32)
    step_dual = lax.scan(back_step, initial, resid_incr, reverse=True)[1]
    target = resid_dual - covariance(step_dual)

    def fore_step(running, right_side):
        running = right_side + forward_apply(model_blocks, model_pattern, running.astype(jnp.bfloat16))
        return running, running

    step_incr = lax.scan(fore_step, initial, target)[1]
    return increment + relax_factor * step_incr, dual_field + relax_factor * step_dual
```

```python
import functools

import jax
import jax.numpy as jnp
from jax import lax
from jax.experimental import pallas as pl
from jax.experimental.pallas import tpu as pltpu
from jax.sharding import PartitionSpec as P

WIN = 8
LEV = 128
SLAB = LEV // WIN
OWN = 1024
BLK = 64
ROWS = OWN // BLK
RU, NNZ_U = 4, 8
RM, NNZ_M = 2, 4
TURN = RM * BLK
HALO = (WIN - 1) * TURN
EXT = OWN + 2 * HALO
END = HALO + OWN
RIM = RU * BLK
M_SIDE = HALO // BLK
M_PAIRS = EXT // 128
FOURS = OWN // 256
EARLY = 3
RELAX = 0.75
MESH = pl.DeviceIdType.MESH
F32 = jnp.float32
BF16 = jnp.bfloat16


def rows_of(window):
    if isinstance(window, int):
        return pl.ds(window * SLAB, SLAB)
    return pl.ds(pl.multiple_of(window * SLAB, SLAB), SLAB)


def lane_index():
    return lax.broadcasted_iota(jnp.int32, (1, 128), 1)


def spread_positions(pattern, first_row, reach, total):
    count = pattern.shape[0]
    own_row = first_row + lax.broadcasted_iota(jnp.int32, (count, ROWS), 1)
    offset = pattern - own_row + reach
    offset = jnp.where(offset < 0, offset + total, offset)
    offset = jnp.where(offset >= total, offset - total, offset)
    offset = jnp.transpose(offset.astype(F32))
    low = lax.broadcasted_iota(jnp.int32, (ROWS, 128), 1) < BLK
    spread = []
    for pair in range(count // 2):
        even = jnp.broadcast_to(offset[:, 2 * pair : 2 * pair + 1], (ROWS, 128))
        odd = jnp.broadcast_to(offset[:, 2 * pair + 1 : 2 * pair + 2], (ROWS, 128))
        spread.append(jnp.where(low, even, odd))
        spread.append(jnp.where(low, odd, even))
    return spread


def place_row(raw, positions, count, first_position):
    terms = []
    for pair in range(raw.shape[1] // 128):
        part = raw[:, pair * 128 : (pair + 1) * 128]
        turned = pltpu.roll(part.astype(F32), BLK, 1).astype(BF16)
        terms.append((part, positions[2 * pair]))
        terms.append((turned, positions[2 * pair + 1]))
    upper = (lane_index() >= BLK).astype(jnp.int32)
    tiles = []
    for v in range(count):
        wanted = (first_position + 2 * v + upper).astype(F32)
        total = None
        for part, position in terms:
            mask = jnp.broadcast_to((position == wanted).astype(F32), (16, 128)).astype(BF16)
            term = part * jnp.concatenate([mask] * (BLK // 16), axis=0)
            total = term if total is None else total + term
        tiles.append(total)
    return tiles


def weights(band, m):
    return jnp.concatenate(
        [band[m - 1 + s, :, 384 - 128 * s : 640 - 128 * s] for s in range(4)], axis=0
    )


def split(value):
    high = value.astype(BF16)
    return high, (value - high.astype(F32)).astype(BF16)


def kernel(
    ncol,
    inc,
    dep,
    og,
    ow,
    es,
    cb,
    cp,
    mb,
    mp,
    x_out,
    d_out,
    inc_v,
    og_v,
    ow_v,
    dep_v,
    es_v,
    g_t,
    dep_t,
    es_t,
    g_f,
    dep_f,
    es_f,
    d_f,
    d_lo,
    s_f,
    p_out,
    p_in,
    i_f,
    t_own,
    t_f,
    x_f,
    x_lo,
    x_r,
    d_r,
    m_raw,
    c_raw,
    m_pat,
    c_pat,
    m_pos,
    c_pos,
    m_band,
    m_turn,
    u_band,
    local_sem,
    g_send,
    g_recv,
    es_send,
    es_recv,
    dep_send,
    dep_recv,
    dr_send,
    dr_recv,
    xr_send,
    xr_recv,
    side_send,
    side_recv,
    gh_send,
    gh_recv,
    p_send,
    p_recv,
    th_send,
    th_recv,
):
    me = lax.axis_index("win")
    col = lax.axis_index("col")
    left = lax.rem(col + ncol - 1, ncol)
    right = lax.rem(col + 1, ncol)
    sides = (left, right)
    total_blocks = ncol * ROWS
    own_cols = pl.ds(HALO, OWN)
    whole = pl.ds(0, OWN)
    every = pl.ds(0, 128)
    sent, due = [], {}

    def to_window(src, dst, send, recv, window):
        return pltpu.make_async_remote_copy(
            src_ref=src, dst_ref=dst, send_sem=send, recv_sem=recv,
            device_id=(window, col), device_id_type=MESH,
        )

    def to_side(src, dst, send, recv, side):
        return pltpu.make_async_remote_copy(
            src_ref=src, dst_ref=dst, send_sem=send, recv_sem=recv,
            device_id=(me, sides[side]), device_id_type=MESH,
        )

    def arrive(*key):
        due.pop(key)()

    def start_sides(key, copies):
        for copy in copies:
            copy.start()
            sent.append(copy.wait_send)
        due[key] = lambda: [copy.wait_recv() for copy in copies]

    def give_out(name, src, dst, cols, sends, recvs):
        for d in range(1, WIN):
            window = lax.rem(me + d, WIN)
            to_window(
                src.at[rows_of(window), :], dst.at[rows_of(me), cols], sends.at[window], recvs.at[me], window
            ).start()
        for k in range(WIN):
            def slab(k=k):
                return to_window(
                    src.at[rows_of(k), :], dst.at[rows_of(k), cols], sends.at[k], recvs.at[k], k
                )

            def sent_slab(slab=slab, k=k):
                @pl.when(me != k)
                def _():
                    slab().wait_send()

            def due_slab(slab=slab, k=k):
                @pl.when(me != k)
                def _():
                    slab().wait_recv()

            sent.append(sent_slab)
            due[name, k] = due_slab

    def give_back(name, src, dst, k, sends, recvs):
        def back():
            return to_window(src.at[rows_of(k), own_cols], dst.at[rows_of(me), :], sends.at[k], recvs.at[me], k)

        @pl.when(me != k)
        def _():
            back().start()

        @pl.when(me == k)
        def _():
            dst[rows_of(me), :] = src[rows_of(k), HALO:END]

        def sent_back():
            @pl.when(me != k)
            def _():
                back().wait_send()

        def due_back():
            @pl.when(me != k)
            def _():
                to_window(dst.at[rows_of(k), :], dst.at[rows_of(k), :], sends.at[k], recvs.at[k], k).wait_recv()

        sent.append(sent_back)
        due[name, k] = due_back

    def halo_copies(src, window, width, sends, recvs):
        rows = rows_of(window)
        return (
            to_side(
                src.at[rows, pl.ds(HALO, width)], src.at[rows, pl.ds(END, width)],
                sends.at[window, 0], recvs.at[window, 0], 0,
            ),
            to_side(
                src.at[rows, pl.ds(END - width, width)], src.at[rows, pl.ds(HALO - width, width)],
                sends.at[window, 1], recvs.at[window, 1], 1,
            ),
        )

    def close():
        for key in list(due):
            arrive(*key)
        for wait in sent:
            wait()

    barrier = pltpu.get_barrier_semaphore()
    for d in range(1, WIN):
        pl.semaphore_signal(barrier, inc=1, device_id=(lax.rem(me + d, WIN), col), device_id_type=MESH)
    for side in range(2):
        pl.semaphore_signal(barrier, inc=1, device_id=(me, sides[side]), device_id_type=MESH)

    loads = [
        pltpu.make_async_copy(inc.at[0], inc_v, local_sem.at[0]),
        pltpu.make_async_copy(og.at[0], og_v, local_sem.at[1]),
        pltpu.make_async_copy(ow.at[0], ow_v, local_sem.at[2]),
        pltpu.make_async_copy(es, es_v, local_sem.at[3]),
        pltpu.make_async_copy(mp, m_pat.at[1], local_sem.at[4]),
        pltpu.make_async_copy(cp, c_pat, local_sem.at[5]),
        pltpu.make_async_copy(mb, m_raw.at[pl.ds(ROWS, ROWS)], local_sem.at[6]),
        pltpu.make_async_copy(cb, c_raw, local_sem.at[7]),
        pltpu.make_async_copy(dep.at[0], dep_v, local_sem.at[8]),
    ]
    for load in loads:
        load.start()
    for load in loads[:4]:
        load.wait()
    for c in range(OWN // 128):
        at = slice(c * 128, (c + 1) * 128)
        g = ow_v[at, :].astype(F32) * inc_v[at, :] - og_v[at, :]
        g_t[:, at] = jnp.transpose(g).astype(BF16)
    es_t[...] = jnp.transpose(jnp.broadcast_to(es_v[...], (128, LEV)))

    pl.semaphore_wait(barrier, WIN + 1)

    give_out("g", g_t, g_f, own_cols, g_send, g_recv)
    n = M_SIDE
    start_sides(
        ("pattern",),
        (
            to_side(mp, m_pat.at[2], side_send.at[0, 0], side_recv.at[0, 0], 0),
            to_side(mp, m_pat.at[0], side_send.at[0, 1], side_recv.at[0, 1], 1),
        ),
    )
    start_sides(
        ("blocks",),
        (
            to_side(mb.at[pl.ds(0, n)], m_raw.at[pl.ds(2 * ROWS, n)], side_send.at[1, 0], side_recv.at[1, 0], 0),
            to_side(mb.at[pl.ds(ROWS - n, n)], m_raw.at[pl.ds(ROWS - n, n)], side_send.at[1, 1], side_recv.at[1, 1], 1),
        ),
    )
    give_out("es", es_t, es_f, every, es_send, es_recv)
    g_f[rows_of(me), HALO:END] = g_t[rows_of(me), :]
    es_f[rows_of(me), :] = es_t[rows_of(me), :]

    def store_positions(side):
        where = slice(side * ROWS, (side + 1) * ROWS)
        block = (left, col, right)[side] * ROWS
        for n, value in enumerate(spread_positions(m_pat[side], block, RM, total_blocks)):
            m_pos[n, where, :] = value

    def build_m(first, last):
        def pair(q, carry):
            zero = jnp.zeros((128, 128), BF16)
            m_band[q, :, 0:128] = zero
            m_band[q, :, 512:640] = zero
            for half in range(2):
                row = 2 * q + (ROWS - M_SIDE) + half
                positions = [m_pos[n, pl.ds(row, 1), :] for n in range(NNZ_M)]
                tiles = place_row(m_raw[row], positions, 3, -half)
                for v, tile in enumerate(tiles):
                    m_band[q, half * BLK : (half + 1) * BLK, (v + 1) * 128 : (v + 2) * 128] = tile
            return carry

        lax.fori_loop(first, last, pair, 0)

    def build_u():
        def four(r, carry):
            zero = jnp.zeros((BLK, 128), BF16)
            for sub in range(4):
                row = 4 * r + sub
                where = slice(sub * BLK, (sub + 1) * BLK)
                positions = [c_pos[n, pl.ds(row, 1), :] for n in range(NNZ_U)]
                start = sub // 2
                tiles = place_row(c_raw[row], positions, 5, 2 * start - sub)
                for v, tile in enumerate(tiles):
                    u_band[r, where, (v + start) * 128 : (v + start + 1) * 128] = tile
                u_band[r, where, 5 * (1 - start) * 128 : (5 * (1 - start) + 1) * 128] = zero
            return carry

        lax.fori_loop(0, FOURS, four, 0)

    def turn_tile(p, q_shift):
        tile = m_band[p + q_shift, :, 256 - 128 * q_shift : 384 - 128 * q_shift]
        at = 256 + 128 * q_shift
        m_turn[p, :, at : at + 128] = jnp.transpose(tile)

    def build_turn():
        zero = jnp.zeros((128, 128), BF16)

        def one(p, carry):
            m_turn[p, :, 0:128] = zero
            m_turn[p, :, 512:640] = zero
            for q_shift in (-1, 0, 1):
                turn_tile(p, q_shift)
            return carry

        lax.fori_loop(1, M_PAIRS - 1, one, 0)
        for p, shifts in ((0, (0, 1)), (M_PAIRS - 1, (-1, 0))):
            for v in range(5):
                m_turn[p, :, v * 128 : (v + 1) * 128] = zero
            for q_shift in shifts:
                turn_tile(p, q_shift)

    for load in loads[4:8]:
        load.wait()
    store_positions(1)
    for n, value in enumerate(spread_positions(c_pat[...], col * ROWS, RU, total_blocks)):
        c_pos[n] = value
    side_pairs = M_SIDE // 2
    build_m(side_pairs, side_pairs + ROWS // 2)
    build_u()
    loads[8].wait()
    for c in range(OWN // 128):
        at = slice(c * 128, (c + 1) * 128)
        dep_t[:, at] = jnp.transpose(dep_v[at, :]).astype(BF16)
    for k in range(WIN - 1, -1, -1):
        arrive("g", k)
        if k:
            start_sides(("g halo", k), halo_copies(g_f, k, TURN * k, gh_send, gh_recv))
    give_out("dep", dep_t, dep_f, whole, dep_send, dep_recv)
    dep_f[rows_of(me), :] = dep_t[rows_of(me), :]
    arrive("pattern")
    store_positions(0)
    store_positions(2)
    arrive("blocks")
    build_m(0, side_pairs)
    build_m(side_pairs + ROWS // 2, M_PAIRS)
    for k in range(WIN):
        arrive("es", k)

    def scaled(k):
        scale = jnp.concatenate([es_f[rows_of(k), :]] * 2, axis=1)
        return lambda value: (scale * value).astype(BF16)

    def transposed(rows, c):
        total = None
        for r in range(max(c - 1, 0), min(c + 2, FOURS)):
            at = (c - r + 1) * 256
            term = jnp.dot(
                s_f[rows, r * 256 : (r + 1) * 256], u_band[r, :, at : at + 256], preferred_element_type=F32
            )
            total = term if total is None else total + term
        return total

    def send_rims(part, rows):
        for side, groups in ((0, (-1, 0)), (1, (FOURS - 1, FOURS))):
            for n, c in enumerate(groups):
                p_out[side, rows, n * 256 : (n + 1) * 256] = transposed(rows, c).astype(BF16)
        start_sides(
            ("rims", part),
            tuple(
                to_side(p_out.at[side, rows, :], p_in.at[1 - side, rows, :], p_send.at[part, side], p_recv.at[part, side], side)
                for side in range(2)
            ),
        )

    last = WIN - 1
    arrive("g halo", last)
    d_f[rows_of(last), :] = g_f[rows_of(last), :]
    give_back("d", d_f, d_r, last, dr_send, dr_recv)
    scale = scaled(last)
    for r in range(FOURS):
        s_f[rows_of(last), r * 256 : (r + 1) * 256] = scale(
            g_f[rows_of(last), HALO + r * 256 : HALO + (r + 1) * 256].astype(F32)
        )
    for k in range(last - 1, -1, -1):
        if k:
            arrive("g halo", k)
        scale = jnp.concatenate([es_f[rows_of(k), :]] * 2, axis=1)
        for group in range(OWN // 256 + k):
            m = M_SIDE // 2 - k + 2 * group
            at = slice(m * 128, (m + 2) * 128)
            near = slice((m - 1) * 128, (m + 3) * 128)
            field = d_f[rows_of(k + 1), near]
            if k + 1 < last:
                field = jnp.concatenate([field, d_lo[rows_of(k + 1), near]], axis=0)
            product = jnp.dot(field, weights(m_band, m), preferred_element_type=F32)
            if k + 1 < last:
                product = product[:SLAB] + product[SLAB:]
            value = g_f[rows_of(k), at].astype(F32) + product
            d_f[rows_of(k), at], d_lo[rows_of(k), at] = split(value)
            value = (scale * value).astype(BF16)
            for n in range(2):
                c = m + n - M_SIDE // 2
                if 0 <= c < OWN // 128:
                    s_f[rows_of(k), c * 128 : (c + 1) * 128] = value[:, n * 128 : (n + 1) * 128]
        give_back("d", d_f, d_r, k, dr_send, dr_recv)
        if k == EARLY:
            send_rims(0, slice(EARLY * SLAB, LEV))
    send_rims(1, slice(0, EARLY * SLAB))

    every_row = slice(0, LEV)
    inner = {c: transposed(every_row, c) for c in range(1, FOURS - 1)}
    for c in inner:
        i_f[:, (c + 1) * 256 : (c + 2) * 256] = inner[c].astype(BF16)
    build_turn()
    for k in range(WIN):
        arrive("dep", k)
    arrive("rims", 0)
    arrive("rims", 1)
    for side, groups in ((0, (-1, 0)), (1, (FOURS - 1, FOURS))):
        for n, c in enumerate(groups):
            there = p_in[side, :, n * 256 : (n + 1) * 256].astype(F32)
            i_f[:, (c + 1) * 256 : (c + 2) * 256] = (transposed(every_row, c) + there).astype(BF16)
    scale = es_f[...]
    scale = jnp.concatenate([scale, scale], axis=1)
    for r in range(FOURS):
        product = lax.dot_general(
            i_f[:, r * 256 : r * 256 + 768], u_band[r], (((1,), (1,)), ((), ())), preferred_element_type=F32
        )
        at = slice(r * 256, (r + 1) * 256)
        value = dep_f[:, at].astype(F32) - scale * product
        t_own[:, at] = value
        t_f[:, HALO + r * 256 : HALO + (r + 1) * 256] = value.astype(BF16)

    for k in range(WIN - 1):
        start_sides(("t halo", k), halo_copies(t_f, k, HALO - TURN * k, th_send, th_recv))

    def target(k, m):
        c = m - M_SIDE // 2
        if 0 <= c < OWN // 128:
            return t_own[rows_of(k), c * 128 : (c + 1) * 128]
        return t_f[rows_of(k), m * 128 : (m + 1) * 128].astype(F32)

    for c in range(OWN // 128):
        at = slice(HALO + c * 128, HALO + (c + 1) * 128)
        x_f[rows_of(0), at], x_lo[rows_of(0), at] = split(t_own[rows_of(0), c * 128 : (c + 1) * 128])
    give_back("x", x_f, x_r, 0, xr_send, xr_recv)
    arrive("t halo", 0)
    for at in (slice(0, HALO), slice(END, EXT)):
        x_f[rows_of(0), at] = t_f[rows_of(0), at]
        x_lo[rows_of(0), at] = jnp.zeros((SLAB, HALO), BF16)
    for k in range(1, WIN):
        if k < WIN - 1:
            arrive("t halo", k)
        for group in range(OWN // 256 + WIN - 1 - k):
            m = k + 2 * group
            at = slice(m * 128, (m + 2) * 128)
            near = slice((m - 1) * 128, (m + 3) * 128)
            field = jnp.concatenate([x_f[rows_of(k - 1), near], x_lo[rows_of(k - 1), near]], axis=0)
            product = jnp.dot(field, weights(m_turn, m), preferred_element_type=F32)
            base = jnp.concatenate([target(k, m), target(k, m + 1)], axis=1)
            x_f[rows_of(k), at], x_lo[rows_of(k), at] = split(base + product[:SLAB] + product[SLAB:])
        give_back("x", x_f, x_r, k, xr_send, xr_recv)

    def finish(name, result, out):
        for k in range(WIN):
            arrive(name, k)
        for c in range(OWN // 128):
            at = slice(c * 128, (c + 1) * 128)
            out[at, :] = jnp.transpose(result[:, at].astype(F32)).astype(BF16)

    finish("d", d_r, d_out)
    finish("x", x_r, x_out)
    close()


def body(
    increment,
    dual_field,
    departure,
    obs_grad,
    obs_weight,
    error_scale,
    corr_blocks,
    corr_pattern,
    model_blocks,
    model_pattern,
):
    ncol = lax.axis_size("col")
    vmem = pltpu.VMEM
    dma = pltpu.SemaphoreType.DMA
    hbm = pl.BlockSpec(memory_space=pltpu.HBM)
    x_new, d_new = pl.pallas_call(
        functools.partial(kernel, ncol),
        out_shape=[jax.ShapeDtypeStruct((OWN, LEV), BF16)] * 2,
        in_specs=[hbm] * 9,
        out_specs=[pl.BlockSpec(memory_space=pltpu.VMEM)] * 2,
        scratch_shapes=[
            vmem((OWN, LEV), F32),
            vmem((OWN, LEV), F32),
            vmem((OWN, LEV), BF16),
            vmem((OWN, LEV), F32),
            vmem((1, LEV), F32),
            vmem((LEV, OWN), BF16),
            vmem((LEV, OWN), BF16),
            vmem((LEV, 128), F32),
            vmem((LEV, EXT), BF16),
            vmem((LEV, OWN), BF16),
            vmem((LEV, 128), F32),
            vmem((LEV, EXT), BF16),
            vmem((LEV, EXT), BF16),
            vmem((LEV, OWN), BF16),
            vmem((2, LEV, 2 * RIM), BF16),
            vmem((2, LEV, 2 * RIM), BF16),
            vmem((LEV, OWN + 2 * RIM), BF16),
            vmem((LEV, OWN), F32),
            vmem((LEV, EXT), BF16),
            vmem((LEV, EXT), BF16),
            vmem((LEV, EXT), BF16),
            vmem((LEV, OWN), BF16),
            vmem((LEV, OWN), BF16),
            vmem((3 * ROWS, BLK, NNZ_M * BLK), BF16),
            vmem((ROWS, BLK, NNZ_U * BLK), BF16),
            vmem((3, NNZ_M, ROWS), jnp.int32),
            vmem((NNZ_U, ROWS), jnp.int32),
            vmem((NNZ_M, 3 * ROWS, 128), F32),
            vmem((NNZ_U, ROWS, 128), F32),
            vmem((M_PAIRS, 128, 640), BF16),
            vmem((M_PAIRS, 128, 640), BF16),
            vmem((FOURS, 256, 768), BF16),
            dma((9,)),
        ]
        + [dma((WIN,))] * 10
        + [dma((2, 2))] * 2
        + [dma((WIN, 2))] * 2
        + [dma((2, 2))] * 2
        + [dma((WIN, 2))] * 2,
        compiler_params=pltpu.CompilerParams(
            collective_id=0, has_side_effects=True, vmem_limit_bytes=56 * 1024 * 1024
        ),
    )(
        increment,
        departure,
        obs_grad,
        obs_weight,
        error_scale,
        corr_blocks,
        corr_pattern.T,
        model_blocks,
        model_pattern.T,
    )
    increment_next = (1.0 - RELAX) * increment + RELAX * x_new.astype(F32)[None]
    dual_next = (1.0 - RELAX) * dual_field + RELAX * d_new.astype(F32)[None]
    return increment_next, dual_next


def solution(mesh):
    field = P("win", "col", None)
    return jax.shard_map(
        body,
        mesh=mesh,
        in_specs=(
            field,
            field,
            field,
            field,
            field,
            P("win", None),
            P("col", None, None),
            P("col", None),
            P("col", None, None),
            P("col", None),
        ),
        out_specs=(field, field),
        check_vma=False,
    )
```

```python
import functools

import jax
import jax.numpy as jnp
from jax import lax
from jax.experimental import pallas as pl
from jax.experimental.pallas import tpu as pltpu
from jax.sharding import PartitionSpec as P

WIN = 8
LEV = 128
SLAB = LEV // WIN
OWN = 1024
BLK = 64
ROWS = OWN // BLK
RU, NNZ_U = 4, 8
RM, NNZ_M = 2, 4
TURN = RM * BLK
HALO = (WIN - 1) * TURN
EXT = OWN + 2 * HALO
END = HALO + OWN
RIM = RU * BLK
M_SIDE = HALO // BLK
M_PAIRS = EXT // 128
FOURS = OWN // 256
EARLY = 3
RELAX = 0.75
MESH = pl.DeviceIdType.MESH
F32 = jnp.float32
BF16 = jnp.bfloat16


def rows_of(window):
    if isinstance(window, int):
        return pl.ds(window * SLAB, SLAB)
    return pl.ds(pl.multiple_of(window * SLAB, SLAB), SLAB)


def lane_index():
    return lax.broadcasted_iota(jnp.int32, (1, 128), 1)


def spread_positions(pattern, first_row, reach, total):
    count = pattern.shape[0]
    own_row = first_row + lax.broadcasted_iota(jnp.int32, (count, ROWS), 1)
    offset = pattern - own_row + reach
    offset = jnp.where(offset < 0, offset + total, offset)
    offset = jnp.where(offset >= total, offset - total, offset)
    offset = jnp.transpose(offset.astype(F32))
    low = lax.broadcasted_iota(jnp.int32, (ROWS, 128), 1) < BLK
    spread = []
    for pair in range(count // 2):
        even = jnp.broadcast_to(offset[:, 2 * pair : 2 * pair + 1], (ROWS, 128))
        odd = jnp.broadcast_to(offset[:, 2 * pair + 1 : 2 * pair + 2], (ROWS, 128))
        spread.append(jnp.where(low, even, odd))
        spread.append(jnp.where(low, odd, even))
    return spread


def place_row(raw, positions, count, first_position):
    terms = []
    for pair in range(raw.shape[1] // 128):
        part = raw[:, pair * 128 : (pair + 1) * 128]
        turned = pltpu.roll(part.astype(F32), BLK, 1).astype(BF16)
        terms.append((part, positions[2 * pair]))
        terms.append((turned, positions[2 * pair + 1]))
    upper = (lane_index() >= BLK).astype(jnp.int32)
    tiles = []
    for v in range(count):
        wanted = (first_position + 2 * v + upper).astype(F32)
        total = None
        for part, position in terms:
            mask = jnp.broadcast_to((position == wanted).astype(F32), (16, 128)).astype(BF16)
            term = part * jnp.concatenate([mask] * (BLK // 16), axis=0)
            total = term if total is None else total + term
        tiles.append(total)
    return tiles


def weights(band, m):
    return jnp.concatenate(
        [band[m - 1 + s, :, 384 - 128 * s : 640 - 128 * s] for s in range(4)], axis=0
    )


def split(value):
    high = value.astype(BF16)
    return high, (value - high.astype(F32)).astype(BF16)


def kernel(
    ncol,
    inc,
    dep,
    og,
    ow,
    es,
    cb,
    cp,
    mb,
    mp,
    x_out,
    d_out,
    inc_v,
    og_v,
    ow_v,
    dep_v,
    es_v,
    g_t,
    dep_t,
    es_t,
    g_f,
    dep_f,
    es_f,
    d_f,
    d_lo,
    s_f,
    p_out,
    p_in,
    i_f,
    t_own,
    t_f,
    x_f,
    x_lo,
    x_r,
    d_r,
    m_raw,
    c_raw,
    m_pat,
    c_pat,
    m_pos,
    c_pos,
    m_band,
    m_turn,
    u_band,
    local_sem,
    g_send,
    g_recv,
    es_send,
    es_recv,
    dep_send,
    dep_recv,
    dr_send,
    dr_recv,
    xr_send,
    xr_recv,
    side_send,
    side_recv,
    gh_send,
    gh_recv,
    p_send,
    p_recv,
    th_send,
    th_recv,
):
    me = lax.axis_index("win")
    col = lax.axis_index("col")
    left = lax.rem(col + ncol - 1, ncol)
    right = lax.rem(col + 1, ncol)
    sides = (left, right)
    partner = me + 1 - 2 * lax.rem(me, 2)
    total_blocks = ncol * ROWS
    own_cols = pl.ds(HALO, OWN)
    whole = pl.ds(0, OWN)
    every = pl.ds(0, 128)
    sent, due = [], {}

    def to_window(src, dst, send, recv, window):
        return pltpu.make_async_remote_copy(
            src_ref=src, dst_ref=dst, send_sem=send, recv_sem=recv,
            device_id=(window, col), device_id_type=MESH,
        )

    def to_side(src, dst, send, recv, side, window=me):
        return pltpu.make_async_remote_copy(
            src_ref=src, dst_ref=dst, send_sem=send, recv_sem=recv,
            device_id=(window, sides[side]), device_id_type=MESH,
        )

    def arrive(*key):
        due.pop(key)()

    def start_sides(key, copies):
        for copy in copies:
            copy.start()
            sent.append(copy.wait_send)
        due[key] = lambda: [copy.wait_recv() for copy in copies]

    def give_out(name, src, dst, cols, sends, recvs):
        for d in range(1, WIN):
            window = lax.rem(me + d, WIN)
            to_window(
                src.at[rows_of(window), :], dst.at[rows_of(me), cols], sends.at[window], recvs.at[me], window
            ).start()
        for k in range(WIN):
            def slab(k=k):
                return to_window(
                    src.at[rows_of(k), :], dst.at[rows_of(k), cols], sends.at[k], recvs.at[k], k
                )

            def sent_slab(slab=slab, k=k):
                @pl.when(me != k)
                def _():
                    slab().wait_send()

            def due_slab(slab=slab, k=k):
                @pl.when(me != k)
                def _():
                    slab().wait_recv()

            sent.append(sent_slab)
            due[name, k] = due_slab

    def give_back(name, src, dst, k, sends, recvs):
        def back():
            return to_window(src.at[rows_of(k), own_cols], dst.at[rows_of(me), :], sends.at[k], recvs.at[me], k)

        @pl.when(me != k)
        def _():
            back().start()

        @pl.when(me == k)
        def _():
            dst[rows_of(me), :] = src[rows_of(k), HALO:END]

        def sent_back():
            @pl.when(me != k)
            def _():
                back().wait_send()

        sent.append(sent_back)

    def due_back(name, dst, sends, recvs, here):
        def back(k):
            @pl.when((me != k) & here)
            def _():
                to_window(dst.at[rows_of(k), :], dst.at[rows_of(k), :], sends.at[k], recvs.at[k], k).wait_recv()

        for k in range(WIN):
            due[name, k] = lambda k=k: back(k)

    def halo_copies(src, window, width, sends, recvs):
        rows = rows_of(window)
        return (
            to_side(
                src.at[rows, pl.ds(HALO, width)], src.at[rows, pl.ds(END, width)],
                sends.at[window, 0], recvs.at[window, 0], 0,
            ),
            to_side(
                src.at[rows, pl.ds(END - width, width)], src.at[rows, pl.ds(HALO - width, width)],
                sends.at[window, 1], recvs.at[window, 1], 1,
            ),
        )

    def close():
        for key in list(due):
            arrive(*key)
        for wait in sent:
            wait()

    barrier = pltpu.get_barrier_semaphore()
    for d in range(1, WIN):
        pl.semaphore_signal(barrier, inc=1, device_id=(lax.rem(me + d, WIN), col), device_id_type=MESH)
    for window in (me, partner):
        for side in range(2):
            pl.semaphore_signal(barrier, inc=1, device_id=(window, sides[side]), device_id_type=MESH)

    loads = [
        pltpu.make_async_copy(inc.at[0], inc_v, local_sem.at[0]),
        pltpu.make_async_copy(og.at[0], og_v, local_sem.at[1]),
        pltpu.make_async_copy(ow.at[0], ow_v, local_sem.at[2]),
        pltpu.make_async_copy(es, es_v, local_sem.at[3]),
        pltpu.make_async_copy(mp, m_pat.at[1], local_sem.at[4]),
        pltpu.make_async_copy(cp, c_pat, local_sem.at[5]),
        pltpu.make_async_copy(mb, m_raw.at[pl.ds(ROWS, ROWS)], local_sem.at[6]),
        pltpu.make_async_copy(cb, c_raw, local_sem.at[7]),
        pltpu.make_async_copy(dep.at[0], dep_v, local_sem.at[8]),
    ]
    for load in loads:
        load.start()
    for load in loads[:4]:
        load.wait()
    for c in range(OWN // 128):
        at = slice(c * 128, (c + 1) * 128)
        g = ow_v[at, :].astype(F32) * inc_v[at, :] - og_v[at, :]
        g_t[:, at] = jnp.transpose(g).astype(BF16)
    es_t[...] = jnp.transpose(jnp.broadcast_to(es_v[...], (128, LEV)))

    pl.semaphore_wait(barrier, WIN - 1 + 4)

    give_out("g", g_t, g_f, own_cols, g_send, g_recv)
    start_sides(
        ("pattern",),
        (
            to_side(mp, m_pat.at[2], side_send.at[0, 0], side_recv.at[0, 0], 0),
            to_side(mp, m_pat.at[0], side_send.at[0, 1], side_recv.at[0, 1], 1),
        ),
    )
    half = M_SIDE // 2
    across = (lax.rem(col, ncol // 2) == 0, lax.rem(col + 1, ncol // 2) == 0)
    for part in range(2):
        copies = []
        for side, first in ((0, part * half), (1, ROWS - M_SIDE + part * half)):
            rows = (pl.ds(2 * ROWS + first, half), pl.ds(first, half))[side]
            window = jnp.where(across[side], partner, me) if part else me
            copies.append(
                to_side(
                    mb.at[pl.ds(first, half)], m_raw.at[rows],
                    side_send.at[1 + part, side], side_recv.at[1 + part, side], side, window,
                )
            )
        start_sides(("blocks", part), tuple(copies))
    give_out("es", es_t, es_f, every, es_send, es_recv)
    g_f[rows_of(me), HALO:END] = g_t[rows_of(me), :]
    es_f[rows_of(me), :] = es_t[rows_of(me), :]

    loads[8].wait()
    for c in range(OWN // 128):
        at = slice(c * 128, (c + 1) * 128)
        dep_t[:, at] = jnp.transpose(dep_v[at, :]).astype(BF16)
    give_out("dep", dep_t, dep_f, whole, dep_send, dep_recv)
    dep_f[rows_of(me), :] = dep_t[rows_of(me), :]

    def store_positions(side):
        where = slice(side * ROWS, (side + 1) * ROWS)
        block = (left, col, right)[side] * ROWS
        for n, value in enumerate(spread_positions(m_pat[side], block, RM, total_blocks)):
            m_pos[n, where, :] = value

    def build_m(first, last):
        def pair(q, carry):
            zero = jnp.zeros((128, 128), BF16)
            m_band[q, :, 0:128] = zero
            m_band[q, :, 512:640] = zero
            for half in range(2):
                row = 2 * q + (ROWS - M_SIDE) + half
                positions = [m_pos[n, pl.ds(row, 1), :] for n in range(NNZ_M)]
                tiles = place_row(m_raw[row], positions, 3, -half)
                for v, tile in enumerate(tiles):
                    m_band[q, half * BLK : (half + 1) * BLK, (v + 1) * 128 : (v + 2) * 128] = tile
            return carry

        lax.fori_loop(first, last, pair, 0)

    def build_u():
        def four(r, carry):
            zero = jnp.zeros((BLK, 128), BF16)
            for sub in range(4):
                row = 4 * r + sub
                where = slice(sub * BLK, (sub + 1) * BLK)
                positions = [c_pos[n, pl.ds(row, 1), :] for n in range(NNZ_U)]
                start = sub // 2
                tiles = place_row(c_raw[row], positions, 5, 2 * start - sub)
                for v, tile in enumerate(tiles):
                    u_band[r, where, (v + start) * 128 : (v + start + 1) * 128] = tile
                u_band[r, where, 5 * (1 - start) * 128 : (5 * (1 - start) + 1) * 128] = zero
            return carry

        lax.fori_loop(0, FOURS, four, 0)

    def turn_tile(p, q_shift):
        tile = m_band[p + q_shift, :, 256 - 128 * q_shift : 384 - 128 * q_shift]
        at = 256 + 128 * q_shift
        m_turn[p, :, at : at + 128] = jnp.transpose(tile)

    def build_turn():
        zero = jnp.zeros((128, 128), BF16)

        def one(p, carry):
            m_turn[p, :, 0:128] = zero
            m_turn[p, :, 512:640] = zero
            for q_shift in (-1, 0, 1):
                turn_tile(p, q_shift)
            return carry

        lax.fori_loop(1, M_PAIRS - 1, one, 0)
        for p, shifts in ((0, (0, 1)), (M_PAIRS - 1, (-1, 0))):
            for v in range(5):
                m_turn[p, :, v * 128 : (v + 1) * 128] = zero
            for q_shift in shifts:
                turn_tile(p, q_shift)

    for load in loads[4:8]:
        load.wait()
    store_positions(1)
    for n, value in enumerate(spread_positions(c_pat[...], col * ROWS, RU, total_blocks)):
        c_pos[n] = value
    side_pairs = M_SIDE // 2
    build_m(side_pairs, side_pairs + ROWS // 2)
    build_u()
    for k in range(WIN - 1, -1, -1):
        arrive("g", k)
        if k:
            start_sides(("g halo", k), halo_copies(g_f, k, TURN * k, gh_send, gh_recv))
    arrive("pattern")
    store_positions(0)
    store_positions(2)
    arrive("blocks", 0)
    arrive("blocks", 1)
    build_m(0, side_pairs)
    build_m(side_pairs + ROWS // 2, M_PAIRS)
    for k in range(WIN):
        arrive("es", k)

    def scaled(k):
        scale = jnp.concatenate([es_f[rows_of(k), :]] * 2, axis=1)
        return lambda value: (scale * value).astype(BF16)

    def transposed(rows, c):
        total = None
        for r in range(max(c - 1, 0), min(c + 2, FOURS)):
            at = (c - r + 1) * 256
            term = jnp.dot(
                s_f[rows, r * 256 : (r + 1) * 256], u_band[r, :, at : at + 256], preferred_element_type=F32
            )
            total = term if total is None else total + term
        return total

    def send_rims(part, rows):
        for side, groups in ((0, (-1, 0)), (1, (FOURS - 1, FOURS))):
            for n, c in enumerate(groups):
                p_out[side, rows, n * 256 : (n + 1) * 256] = transposed(rows, c).astype(BF16)
        start_sides(
            ("rims", part),
            tuple(
                to_side(p_out.at[side, rows, :], p_in.at[1 - side, rows, :], p_send.at[part, side], p_recv.at[part, side], side)
                for side in range(2)
            ),
        )

    last = WIN - 1
    arrive("g halo", last)
    d_f[rows_of(last), :] = g_f[rows_of(last), :]
    scale = scaled(last)
    for r in range(FOURS):
        s_f[rows_of(last), r * 256 : (r + 1) * 256] = scale(
            g_f[rows_of(last), HALO + r * 256 : HALO + (r + 1) * 256].astype(F32)
        )
    for k in range(last - 1, -1, -1):
        if k:
            arrive("g halo", k)
        scale = jnp.concatenate([es_f[rows_of(k), :]] * 2, axis=1)
        for group in range(OWN // 256 + k):
            m = M_SIDE // 2 - k + 2 * group
            at = slice(m * 128, (m + 2) * 128)
            near = slice((m - 1) * 128, (m + 3) * 128)
            field = d_f[rows_of(k + 1), near]
            if k + 1 < last:
                field = jnp.concatenate([field, d_lo[rows_of(k + 1), near]], axis=0)
            product = jnp.dot(field, weights(m_band, m), preferred_element_type=F32)
            if k + 1 < last:
                product = product[:SLAB] + product[SLAB:]
            value = g_f[rows_of(k), at].astype(F32) + product
            d_f[rows_of(k), at], d_lo[rows_of(k), at] = split(value)
            value = (scale * value).astype(BF16)
            for n in range(2):
                c = m + n - M_SIDE // 2
                if 0 <= c < OWN // 128:
                    s_f[rows_of(k), c * 128 : (c + 1) * 128] = value[:, n * 128 : (n + 1) * 128]
        if k == EARLY:
            send_rims(0, slice(EARLY * SLAB, LEV))
    send_rims(1, slice(0, EARLY * SLAB))
    for k in range(last):
        give_back("d", d_f, d_r, k, dr_send, dr_recv)
    due_back("d", d_r, dr_send, dr_recv, me != last)

    every_row = slice(0, LEV)
    inner = {c: transposed(every_row, c) for c in range(1, FOURS - 1)}
    for c in inner:
        i_f[:, (c + 1) * 256 : (c + 2) * 256] = inner[c].astype(BF16)
    build_turn()
    for k in range(WIN):
        arrive("dep", k)
    arrive("rims", 0)
    arrive("rims", 1)
    for side, groups in ((0, (-1, 0)), (1, (FOURS - 1, FOURS))):
        for n, c in enumerate(groups):
            there = p_in[side, :, n * 256 : (n + 1) * 256].astype(F32)
            i_f[:, (c + 1) * 256 : (c + 2) * 256] = (transposed(every_row, c) + there).astype(BF16)
    scale = es_f[...]
    scale = jnp.concatenate([scale, scale], axis=1)
    for r in range(FOURS):
        product = lax.dot_general(
            i_f[:, r * 256 : r * 256 + 768], u_band[r], (((1,), (1,)), ((), ())), preferred_element_type=F32
        )
        at = slice(r * 256, (r + 1) * 256)
        value = dep_f[:, at].astype(F32) - scale * product
        t_own[:, at] = value
        t_f[:, HALO + r * 256 : HALO + (r + 1) * 256] = value.astype(BF16)

    for k in range(WIN - 1):
        start_sides(("t halo", k), halo_copies(t_f, k, HALO - TURN * k, th_send, th_recv))

    def target(k, m):
        c = m - M_SIDE // 2
        if 0 <= c < OWN // 128:
            return t_own[rows_of(k), c * 128 : (c + 1) * 128]
        return t_f[rows_of(k), m * 128 : (m + 1) * 128].astype(F32)

    for c in range(OWN // 128):
        at = slice(HALO + c * 128, HALO + (c + 1) * 128)
        x_f[rows_of(0), at], x_lo[rows_of(0), at] = split(t_own[rows_of(0), c * 128 : (c + 1) * 128])
    give_back("x", x_f, x_r, 0, xr_send, xr_recv)
    arrive("t halo", 0)
    for at in (slice(0, HALO), slice(END, EXT)):
        x_f[rows_of(0), at] = t_f[rows_of(0), at]
        x_lo[rows_of(0), at] = jnp.zeros((SLAB, HALO), BF16)
    for k in range(1, WIN):
        if k < WIN - 1:
            arrive("t halo", k)
        for group in range(OWN // 256 + WIN - 1 - k):
            m = k + 2 * group
            at = slice(m * 128, (m + 2) * 128)
            near = slice((m - 1) * 128, (m + 3) * 128)
            field = jnp.concatenate([x_f[rows_of(k - 1), near], x_lo[rows_of(k - 1), near]], axis=0)
            product = jnp.dot(field, weights(m_turn, m), preferred_element_type=F32)
            base = jnp.concatenate([target(k, m), target(k, m + 1)], axis=1)
            x_f[rows_of(k), at], x_lo[rows_of(k), at] = split(base + product[:SLAB] + product[SLAB:])
        give_back("x", x_f, x_r, k, xr_send, xr_recv)
    due_back("x", x_r, xr_send, xr_recv, me >= 0)

    def finish(name, result, out):
        for k in range(WIN):
            arrive(name, k)
        for c in range(OWN // 128):
            at = slice(c * 128, (c + 1) * 128)
            out[at, :] = jnp.transpose(result[:, at].astype(F32)).astype(BF16)

    @pl.when(me == last)
    def _():
        d_r[...] = g_t[...]

    finish("d", d_r, d_out)
    finish("x", x_r, x_out)
    close()


def body(
    increment,
    dual_field,
    departure,
    obs_grad,
    obs_weight,
    error_scale,
    corr_blocks,
    corr_pattern,
    model_blocks,
    model_pattern,
):
    ncol = lax.axis_size("col")
    vmem = pltpu.VMEM
    dma = pltpu.SemaphoreType.DMA
    hbm = pl.BlockSpec(memory_space=pltpu.HBM)
    x_new, d_new = pl.pallas_call(
        functools.partial(kernel, ncol),
        out_shape=[pltpu.VMEM((OWN, LEV), BF16)] * 2,
        in_specs=[hbm] * 9,
        out_specs=[pl.BlockSpec(memory_space=pltpu.VMEM)] * 2,
        scratch_shapes=[
            vmem((OWN, LEV), F32),
            vmem((OWN, LEV), F32),
            vmem((OWN, LEV), BF16),
            vmem((OWN, LEV), F32),
            vmem((1, LEV), F32),
            vmem((LEV, OWN), BF16),
            vmem((LEV, OWN), BF16),
            vmem((LEV, 128), F32),
            vmem((LEV, EXT), BF16),
            vmem((LEV, OWN), BF16),
            vmem((LEV, 128), F32),
            vmem((LEV, EXT), BF16),
            vmem((LEV, EXT), BF16),
            vmem((LEV, OWN), BF16),
            vmem((2, LEV, 2 * RIM), BF16),
            vmem((2, LEV, 2 * RIM), BF16),
            vmem((LEV, OWN + 2 * RIM), BF16),
            vmem((LEV, OWN), F32),
            vmem((LEV, EXT), BF16),
            vmem((LEV, EXT), BF16),
            vmem((LEV, EXT), BF16),
            vmem((LEV, OWN), BF16),
            vmem((LEV, OWN), BF16),
            vmem((3 * ROWS, BLK, NNZ_M * BLK), BF16),
            vmem((ROWS, BLK, NNZ_U * BLK), BF16),
            vmem((3, NNZ_M, ROWS), jnp.int32),
            vmem((NNZ_U, ROWS), jnp.int32),
            vmem((NNZ_M, 3 * ROWS, 128), F32),
            vmem((NNZ_U, ROWS, 128), F32),
            vmem((M_PAIRS, 128, 640), BF16),
            vmem((M_PAIRS, 128, 640), BF16),
            vmem((FOURS, 256, 768), BF16),
            dma((9,)),
        ]
        + [dma((WIN,))] * 10
        + [dma((3, 2))] * 2
        + [dma((WIN, 2))] * 2
        + [dma((2, 2))] * 2
        + [dma((WIN, 2))] * 2,
        compiler_params=pltpu.CompilerParams(
            collective_id=0, has_side_effects=True, vmem_limit_bytes=56 * 1024 * 1024
        ),
    )(
        increment,
        departure,
        obs_grad,
        obs_weight,
        error_scale,
        corr_blocks,
        corr_pattern.T,
        model_blocks,
        model_pattern.T,
    )
    increment_next = (1.0 - RELAX) * increment + RELAX * x_new.astype(F32)[None]
    dual_next = (1.0 - RELAX) * dual_field + RELAX * d_new.astype(F32)[None]
    return increment_next, dual_next


def solution(mesh):
    field = P("win", "col", None)
    return jax.shard_map(
        body,
        mesh=mesh,
        in_specs=(
            field,
            field,
            field,
            field,
            field,
            P("win", None),
            P("col", None, None),
            P("col", None),
            P("col", None, None),
            P("col", None),
        ),
        out_specs=(field, field),
        check_vma=False,
    )
```

```python
import functools

import jax
import jax.numpy as jnp
from jax import lax
from jax.experimental import pallas as pl
from jax.experimental.pallas import tpu as pltpu
from jax.sharding import PartitionSpec as P

WIN = 8
LEV = 128
SLAB = LEV // WIN
OWN = 1024
BLK = 64
ROWS = OWN // BLK
RU, NNZ_U = 4, 8
RM, NNZ_M = 2, 4
TURN = RM * BLK
HALO = (WIN - 1) * TURN
EXT = OWN + 2 * HALO
END = HALO + OWN
RIM = RU * BLK
M_SIDE = HALO // BLK
M_PAIRS = EXT // 128
FOURS = OWN // 256
EDGES = (-1, 0, FOURS - 1, FOURS)
EARLY = 4
G_GROUPS = ((6, 7), (3, 4, 5), (1, 2))
T_GROUPS = ((0, 1), (2, 3), (4, 5, 6))
RELAX = 0.75
MESH = pl.DeviceIdType.MESH
F32 = jnp.float32
BF16 = jnp.bfloat16


def rows_of(window):
    if isinstance(window, int):
        return pl.ds(window * SLAB, SLAB)
    return pl.ds(pl.multiple_of(window * SLAB, SLAB), SLAB)


def lane_index():
    return lax.broadcasted_iota(jnp.int32, (1, 128), 1)


def spread_positions(pattern, first_row, reach, total):
    count = pattern.shape[0]
    own_row = first_row + lax.broadcasted_iota(jnp.int32, (count, ROWS), 1)
    offset = pattern - own_row + reach
    offset = jnp.where(offset < 0, offset + total, offset)
    offset = jnp.where(offset >= total, offset - total, offset)
    offset = jnp.transpose(offset.astype(F32))
    low = lax.broadcasted_iota(jnp.int32, (ROWS, 128), 1) < BLK
    spread = []
    for pair in range(count // 2):
        even = jnp.broadcast_to(offset[:, 2 * pair : 2 * pair + 1], (ROWS, 128))
        odd = jnp.broadcast_to(offset[:, 2 * pair + 1 : 2 * pair + 2], (ROWS, 128))
        spread.append(jnp.where(low, even, odd))
        spread.append(jnp.where(low, odd, even))
    return spread


def place_row(raw, positions, count, first_position):
    terms = []
    for pair in range(raw.shape[1] // 128):
        part = raw[:, pair * 128 : (pair + 1) * 128]
        turned = pltpu.roll(part.astype(F32), BLK, 1).astype(BF16)
        terms.append((part, positions[2 * pair]))
        terms.append((turned, positions[2 * pair + 1]))
    upper = (lane_index() >= BLK).astype(jnp.int32)
    tiles = []
    for v in range(count):
        wanted = (first_position + 2 * v + upper).astype(F32)
        total = None
        for part, position in terms:
            mask = jnp.broadcast_to((position == wanted).astype(F32), (16, 128)).astype(BF16)
            term = part * jnp.concatenate([mask] * (BLK // 16), axis=0)
            total = term if total is None else total + term
        tiles.append(total)
    return tiles


def weights(band, m):
    return jnp.concatenate(
        [band[m - 1 + s, :, 384 - 128 * s : 640 - 128 * s] for s in range(4)], axis=0
    )


def split(value):
    high = value.astype(BF16)
    return high, (value - high.astype(F32)).astype(BF16)


def kernel(
    ncol,
    inc,
    dep,
    og,
    ow,
    es,
    cb,
    cp,
    mb,
    mp,
    x_out,
    d_out,
    inc_v,
    og_v,
    ow_v,
    dep_v,
    es_v,
    g_t,
    dep_t,
    es_t,
    g_f,
    dep_f,
    es_all,
    es_f,
    d_f,
    d_lo,
    s_f,
    p_out,
    p_in,
    p_own,
    i_f,
    t_own,
    t_f,
    x_f,
    x_lo,
    x_r,
    d_r,
    m_raw,
    c_raw,
    m_pat,
    c_pat,
    m_pos,
    c_pos,
    m_band,
    m_turn,
    u_band,
    local_sem,
    g_send,
    g_recv,
    es_send,
    es_recv,
    dep_send,
    dep_recv,
    dr_send,
    dr_recv,
    xr_send,
    xr_recv,
    side_send,
    side_recv,
    gh_send,
    gh_recv,
    p_send,
    p_recv,
    th_send,
    th_recv,
):
    me = lax.axis_index("win")
    col = lax.axis_index("col")
    left = lax.rem(col + ncol - 1, ncol)
    right = lax.rem(col + 1, ncol)
    sides = (left, right)
    partner = me + 1 - 2 * lax.rem(me, 2)
    total_blocks = ncol * ROWS
    own_cols = pl.ds(HALO, OWN)
    whole = pl.ds(0, OWN)
    sent, due = [], {}

    def to_window(src, dst, send, recv, window):
        return pltpu.make_async_remote_copy(
            src_ref=src, dst_ref=dst, send_sem=send, recv_sem=recv,
            device_id=(window, col), device_id_type=MESH,
        )

    def to_side(src, dst, send, recv, side, window=me):
        return pltpu.make_async_remote_copy(
            src_ref=src, dst_ref=dst, send_sem=send, recv_sem=recv,
            device_id=(window, sides[side]), device_id_type=MESH,
        )

    def arrive(*key):
        due.pop(key)()

    def start_sides(key, copies):
        for copy in copies:
            copy.start()
            sent.append(copy.wait_send)
        due[key] = lambda: [copy.wait_recv() for copy in copies]

    def give_out(name, src, dst, cols, sends, recvs):
        for d in (3, 5, 1, 7, 4, 2, 6):
            window = lax.rem(me + d, WIN)
            to_window(
                src.at[rows_of(window), :], dst.at[rows_of(me), cols], sends.at[window], recvs.at[me], window
            ).start()
        for k in range(WIN):
            def slab(k=k):
                return to_window(
                    src.at[rows_of(k), :], dst.at[rows_of(k), cols], sends.at[k], recvs.at[k], k
                )

            def sent_slab(slab=slab, k=k):
                @pl.when(me != k)
                def _():
                    slab().wait_send()

            def due_slab(slab=slab, k=k):
                @pl.when(me != k)
                def _():
                    slab().wait_recv()

            sent.append(sent_slab)
            due[name, k] = due_slab

    def give_back(name, src, dst, k, sends, recvs):
        def back():
            return to_window(src.at[rows_of(k), own_cols], dst.at[rows_of(me), :], sends.at[k], recvs.at[me], k)

        @pl.when(me != k)
        def _():
            back().start()

        @pl.when(me == k)
        def _():
            dst[rows_of(me), :] = src[rows_of(k), HALO:END]

        def sent_back():
            @pl.when(me != k)
            def _():
                back().wait_send()

        sent.append(sent_back)

    def due_back(name, dst, sends, recvs, here):
        def back(k):
            @pl.when((me != k) & here)
            def _():
                to_window(dst.at[rows_of(k), :], dst.at[rows_of(k), :], sends.at[k], recvs.at[k], k).wait_recv()

        for k in range(WIN):
            due[name, k] = lambda k=k: back(k)

    def halo_copies(src, windows, width, sends, recvs):
        window = windows[0]
        rows = pl.ds(window * SLAB, len(windows) * SLAB)
        return (
            to_side(
                src.at[rows, pl.ds(HALO, width)], src.at[rows, pl.ds(END, width)],
                sends.at[window, 0], recvs.at[window, 0], 0,
            ),
            to_side(
                src.at[rows, pl.ds(END - width, width)], src.at[rows, pl.ds(HALO - width, width)],
                sends.at[window, 1], recvs.at[window, 1], 1,
            ),
        )

    def close():
        for key in list(due):
            arrive(*key)
        for wait in sent:
            wait()

    barrier = pltpu.get_barrier_semaphore()
    for d in range(1, WIN):
        pl.semaphore_signal(barrier, inc=1, device_id=(lax.rem(me + d, WIN), col), device_id_type=MESH)
    for window in (me, partner):
        for side in range(2):
            pl.semaphore_signal(barrier, inc=1, device_id=(window, sides[side]), device_id_type=MESH)

    loads = [
        pltpu.make_async_copy(inc.at[0], inc_v, local_sem.at[0]),
        pltpu.make_async_copy(og.at[0], og_v, local_sem.at[1]),
        pltpu.make_async_copy(ow.at[0], ow_v, local_sem.at[2]),
        pltpu.make_async_copy(es, es_v, local_sem.at[3]),
        pltpu.make_async_copy(mp, m_pat.at[1], local_sem.at[4]),
        pltpu.make_async_copy(cp, c_pat, local_sem.at[5]),
        pltpu.make_async_copy(mb, m_raw.at[pl.ds(ROWS, ROWS)], local_sem.at[6]),
        pltpu.make_async_copy(cb, c_raw, local_sem.at[7]),
        pltpu.make_async_copy(dep.at[0], dep_v, local_sem.at[8]),
    ]
    for load in loads:
        load.start()
    for load in loads[:4]:
        load.wait()
    for c in range(OWN // 128):
        at = slice(c * 128, (c + 1) * 128)
        g = ow_v[at, :].astype(F32) * inc_v[at, :] - og_v[at, :]
        g_t[:, at] = jnp.transpose(g).astype(BF16)

    pl.semaphore_wait(barrier, WIN - 1 + 4)

    give_out("g", g_t, g_f, own_cols, g_send, g_recv)
    start_sides(
        ("pattern",),
        (
            to_side(mp, m_pat.at[2], side_send.at[0, 0], side_recv.at[0, 0], 0),
            to_side(mp, m_pat.at[0], side_send.at[0, 1], side_recv.at[0, 1], 1),
        ),
    )
    half = M_SIDE // 2
    across = (lax.rem(col, ncol // 2) == 0, lax.rem(col + 1, ncol // 2) == 0)
    for part in range(2):
        copies = []
        for side, first in ((0, part * half), (1, ROWS - M_SIDE + part * half)):
            rows = (pl.ds(2 * ROWS + first, half), pl.ds(first, half))[side]
            window = jnp.where(across[side], partner, me) if part else me
            copies.append(
                to_side(
                    mb.at[pl.ds(first, half)], m_raw.at[rows],
                    side_send.at[1 + part, side], side_recv.at[1 + part, side], side, window,
                )
            )
        start_sides(("blocks", part), tuple(copies))
    for d in range(1, WIN):
        window = lax.rem(me + d, WIN)
        to_window(es_v, es_all.at[me], es_send.at[window], es_recv.at[me], window).start()
    for k in range(WIN):
        def scale_row(k=k):
            return to_window(es_v, es_all.at[k], es_send.at[k], es_recv.at[k], k)

        def sent_row(row=scale_row, k=k):
            @pl.when(me != k)
            def _():
                row().wait_send()

        def due_row(row=scale_row, k=k):
            @pl.when(me != k)
            def _():
                row().wait_recv()

        sent.append(sent_row)
        due["es", k] = due_row
    es_all[me] = es_v[...]
    g_f[rows_of(me), HALO:END] = g_t[rows_of(me), :]

    loads[8].wait()
    for c in range(OWN // 128):
        at = slice(c * 128, (c + 1) * 128)
        dep_t[:, at] = jnp.transpose(dep_v[at, :]).astype(BF16)

    def store_positions(side):
        where = slice(side * ROWS, (side + 1) * ROWS)
        block = (left, col, right)[side] * ROWS
        for n, value in enumerate(spread_positions(m_pat[side], block, RM, total_blocks)):
            m_pos[n, where, :] = value

    def build_m(first, last):
        def pair(q, carry):
            zero = jnp.zeros((128, 128), BF16)
            m_band[q, :, 0:128] = zero
            m_band[q, :, 512:640] = zero
            for half in range(2):
                row = 2 * q + (ROWS - M_SIDE) + half
                positions = [m_pos[n, pl.ds(row, 1), :] for n in range(NNZ_M)]
                tiles = place_row(m_raw[row], positions, 3, -half)
                for v, tile in enumerate(tiles):
                    m_band[q, half * BLK : (half + 1) * BLK, (v + 1) * 128 : (v + 2) * 128] = tile
            return carry

        lax.fori_loop(first, last, pair, 0)

    def build_u():
        def four(r, carry):
            zero = jnp.zeros((BLK, 128), BF16)
            for sub in range(4):
                row = 4 * r + sub
                where = slice(sub * BLK, (sub + 1) * BLK)
                positions = [c_pos[n, pl.ds(row, 1), :] for n in range(NNZ_U)]
                start = sub // 2
                tiles = place_row(c_raw[row], positions, 5, 2 * start - sub)
                for v, tile in enumerate(tiles):
                    u_band[r, where, (v + start) * 128 : (v + start + 1) * 128] = tile
                u_band[r, where, 5 * (1 - start) * 128 : (5 * (1 - start) + 1) * 128] = zero
            return carry

        lax.fori_loop(0, FOURS, four, 0)

    def turn_tile(p, q_shift):
        tile = m_band[p + q_shift, :, 256 - 128 * q_shift : 384 - 128 * q_shift]
        at = 256 + 128 * q_shift
        m_turn[p, :, at : at + 128] = jnp.transpose(tile)

    def build_turn():
        zero = jnp.zeros((128, 128), BF16)

        def one(p, carry):
            m_turn[p, :, 0:128] = zero
            m_turn[p, :, 512:640] = zero
            for q_shift in (-1, 0, 1):
                turn_tile(p, q_shift)
            return carry

        lax.fori_loop(1, M_PAIRS - 1, one, 0)
        for p, shifts in ((0, (0, 1)), (M_PAIRS - 1, (-1, 0))):
            for v in range(5):
                m_turn[p, :, v * 128 : (v + 1) * 128] = zero
            for q_shift in shifts:
                turn_tile(p, q_shift)

    for load in loads[4:8]:
        load.wait()
    store_positions(1)
    for n, value in enumerate(spread_positions(c_pat[...], col * ROWS, RU, total_blocks)):
        c_pos[n] = value
    side_pairs = M_SIDE // 2
    build_m(side_pairs, side_pairs + ROWS // 2)
    build_u()
    for k in range(WIN - 1, -1, -1):
        arrive("g", k)
        for windows in G_GROUPS:
            if k == windows[0]:
                start_sides(("g halo", windows[-1]), halo_copies(g_f, windows, TURN * windows[-1], gh_send, gh_recv))
    for k in range(WIN):
        arrive("es", k)
    rows = jnp.concatenate([es_all[k] for k in range(WIN)] + [jnp.zeros((128 - WIN, LEV), F32)], axis=0)
    es_t[...] = jnp.transpose(rows)
    columns = es_t[rows_of(me), :]
    for k in range(WIN):
        es_f[rows_of(k), :] = jnp.broadcast_to(columns[:, k : k + 1], (SLAB, 128))
    arrive("pattern")
    store_positions(0)
    store_positions(2)
    arrive("blocks", 0)
    arrive("blocks", 1)
    build_m(0, side_pairs)
    build_m(side_pairs + ROWS // 2, M_PAIRS)

    give_out("dep", dep_t, dep_f, whole, dep_send, dep_recv)
    dep_f[rows_of(me), :] = dep_t[rows_of(me), :]
    def scaled(k):
        scale = jnp.concatenate([es_f[rows_of(k), :]] * 2, axis=1)
        return lambda value: (scale * value).astype(BF16)

    def transposed(rows, c):
        total = None
        for r in range(max(c - 1, 0), min(c + 2, FOURS)):
            at = (c - r + 1) * 256
            term = jnp.dot(
                s_f[rows, r * 256 : (r + 1) * 256], u_band[r, :, at : at + 256], preferred_element_type=F32
            )
            total = term if total is None else total + term
        return total

    def send_rims(part, rows):
        copies = tuple(
            to_side(p_out.at[side, rows, :], p_in.at[1 - side, rows, :], p_send.at[part, side], p_recv.at[part, side], side)
            for side in range(2)
        )
        for side in range(2):
            for n in range(2):
                p_out[side, rows, n * 256 : (n + 1) * 256] = transposed(rows, EDGES[2 * side + n]).astype(BF16)
            copies[side].start()
            sent.append(copies[side].wait_send)
        due["rims", part] = lambda: [copy.wait_recv() for copy in copies]

    last = WIN - 1
    arrive("g halo", last)
    d_f[rows_of(last), :] = g_f[rows_of(last), :]
    scale = scaled(last)
    for r in range(FOURS):
        s_f[rows_of(last), r * 256 : (r + 1) * 256] = scale(
            g_f[rows_of(last), HALO + r * 256 : HALO + (r + 1) * 256].astype(F32)
        )
    for k in range(last - 1, -1, -1):
        if ("g halo", k) in due:
            arrive("g halo", k)
        scale = jnp.concatenate([es_f[rows_of(k), :]] * 2, axis=1)
        for group in range(OWN // 256 + k):
            m = M_SIDE // 2 - k + 2 * group
            at = slice(m * 128, (m + 2) * 128)
            near = slice((m - 1) * 128, (m + 3) * 128)
            field = d_f[rows_of(k + 1), near]
            if k + 1 < last:
                field = jnp.concatenate([field, d_lo[rows_of(k + 1), near]], axis=0)
            product = jnp.dot(field, weights(m_band, m), preferred_element_type=F32)
            if k + 1 < last:
                product = product[:SLAB] + product[SLAB:]
            value = g_f[rows_of(k), at].astype(F32) + product
            d_f[rows_of(k), at], d_lo[rows_of(k), at] = split(value)
            value = (scale * value).astype(BF16)
            for n in range(2):
                c = m + n - M_SIDE // 2
                if 0 <= c < OWN // 128:
                    s_f[rows_of(k), c * 128 : (c + 1) * 128] = value[:, n * 128 : (n + 1) * 128]
        if k == EARLY:
            send_rims(0, slice(EARLY * SLAB, LEV))
    send_rims(1, slice(0, EARLY * SLAB))

    every_row = slice(0, LEV)
    for c in range(1, FOURS - 1):
        i_f[:, (c + 1) * 256 : (c + 2) * 256] = transposed(every_row, c).astype(BF16)
    for n, c in enumerate(EDGES):
        p_own[:, n * 256 : (n + 1) * 256] = transposed(every_row, c)
    build_turn()
    for k in range(WIN):
        arrive("dep", k)
    arrive("rims", 0)
    arrive("rims", 1)
    for n, c in enumerate(EDGES):
        there = p_in[n // 2, :, (n % 2) * 256 : (n % 2 + 1) * 256].astype(F32)
        i_f[:, (c + 1) * 256 : (c + 2) * 256] = (p_own[:, n * 256 : (n + 1) * 256] + there).astype(BF16)
    scale = es_f[...]
    scale = jnp.concatenate([scale, scale], axis=1)
    for r in range(FOURS):
        product = lax.dot_general(
            i_f[:, r * 256 : r * 256 + 768], u_band[r], (((1,), (1,)), ((), ())), preferred_element_type=F32
        )
        at = slice(r * 256, (r + 1) * 256)
        value = dep_f[:, at].astype(F32) - scale * product
        t_own[:, at] = value
        t_f[:, HALO + r * 256 : HALO + (r + 1) * 256] = value.astype(BF16)
    for k in range(last):
        give_back("d", d_f, d_r, k, dr_send, dr_recv)
    due_back("d", d_r, dr_send, dr_recv, me != last)

    for windows in T_GROUPS:
        start_sides(
            ("t halo", windows[0]), halo_copies(t_f, windows, HALO - TURN * windows[0], th_send, th_recv)
        )

    def target(k, m):
        c = m - M_SIDE // 2
        if 0 <= c < OWN // 128:
            return t_own[rows_of(k), c * 128 : (c + 1) * 128]
        return t_f[rows_of(k), m * 128 : (m + 1) * 128].astype(F32)

    for c in range(OWN // 128):
        at = slice(HALO + c * 128, HALO + (c + 1) * 128)
        x_f[rows_of(0), at], x_lo[rows_of(0), at] = split(t_own[rows_of(0), c * 128 : (c + 1) * 128])
    give_back("x", x_f, x_r, 0, xr_send, xr_recv)
    arrive("t halo", 0)
    for at in (slice(0, HALO), slice(END, EXT)):
        x_f[rows_of(0), at] = t_f[rows_of(0), at]
        x_lo[rows_of(0), at] = jnp.zeros((SLAB, HALO), BF16)
    for k in range(1, WIN):
        if ("t halo", k) in due:
            arrive("t halo", k)
        for group in range(OWN // 256 + WIN - 1 - k):
            m = k + 2 * group
            at = slice(m * 128, (m + 2) * 128)
            near = slice((m - 1) * 128, (m + 3) * 128)
            field = jnp.concatenate([x_f[rows_of(k - 1), near], x_lo[rows_of(k - 1), near]], axis=0)
            product = jnp.dot(field, weights(m_turn, m), preferred_element_type=F32)
            base = jnp.concatenate([target(k, m), target(k, m + 1)], axis=1)
            x_f[rows_of(k), at], x_lo[rows_of(k), at] = split(base + product[:SLAB] + product[SLAB:])
        give_back("x", x_f, x_r, k, xr_send, xr_recv)
    due_back("x", x_r, xr_send, xr_recv, me >= 0)

    def finish(name, result, out):
        for k in range(WIN):
            arrive(name, k)
        for c in range(OWN // 128):
            at = slice(c * 128, (c + 1) * 128)
            out[at, :] = jnp.transpose(result[:, at].astype(F32)).astype(BF16)

    @pl.when(me == last)
    def _():
        d_r[...] = g_t[...]

    finish("d", d_r, d_out)
    for wait in sent:
        wait()
    sent.clear()
    finish("x", x_r, x_out)
    close()


def body(
    increment,
    dual_field,
    departure,
    obs_grad,
    obs_weight,
    error_scale,
    corr_blocks,
    corr_pattern,
    model_blocks,
    model_pattern,
):
    ncol = lax.axis_size("col")
    vmem = pltpu.VMEM
    dma = pltpu.SemaphoreType.DMA
    hbm = pl.BlockSpec(memory_space=pltpu.HBM)
    x_new, d_new = pl.pallas_call(
        functools.partial(kernel, ncol),
        out_shape=[pltpu.VMEM((OWN, LEV), BF16)] * 2,
        in_specs=[hbm] * 9,
        out_specs=[pl.BlockSpec(memory_space=pltpu.VMEM)] * 2,
        scratch_shapes=[
            vmem((OWN, LEV), F32),
            vmem((OWN, LEV), F32),
            vmem((OWN, LEV), BF16),
            vmem((OWN, LEV), F32),
            vmem((1, LEV), F32),
            vmem((LEV, OWN), BF16),
            vmem((LEV, OWN), BF16),
            vmem((LEV, 128), F32),
            vmem((LEV, EXT), BF16),
            vmem((LEV, OWN), BF16),
            vmem((WIN, 1, LEV), F32),
            vmem((LEV, 128), F32),
            vmem((LEV, EXT), BF16),
            vmem((LEV, EXT), BF16),
            vmem((LEV, OWN), BF16),
            vmem((2, LEV, 2 * RIM), BF16),
            vmem((2, LEV, 2 * RIM), BF16),
            vmem((LEV, 4 * RIM), F32),
            vmem((LEV, OWN + 2 * RIM), BF16),
            vmem((LEV, OWN), F32),
            vmem((LEV, EXT), BF16),
            vmem((LEV, EXT), BF16),
            vmem((LEV, EXT), BF16),
            vmem((LEV, OWN), BF16),
            vmem((LEV, OWN), BF16),
            vmem((3 * ROWS, BLK, NNZ_M * BLK), BF16),
            vmem((ROWS, BLK, NNZ_U * BLK), BF16),
            vmem((3, NNZ_M, ROWS), jnp.int32),
            vmem((NNZ_U, ROWS), jnp.int32),
            vmem((NNZ_M, 3 * ROWS, 128), F32),
            vmem((NNZ_U, ROWS, 128), F32),
            vmem((M_PAIRS, 128, 640), BF16),
            vmem((M_PAIRS, 128, 640), BF16),
            vmem((FOURS, 256, 768), BF16),
            dma((9,)),
        ]
        + [dma((WIN,))] * 10
        + [dma((3, 2))] * 2
        + [dma((WIN, 2))] * 2
        + [dma((2, 2))] * 2
        + [dma((WIN, 2))] * 2,
        compiler_params=pltpu.CompilerParams(
            collective_id=0, has_side_effects=True, vmem_limit_bytes=56 * 1024 * 1024
        ),
    )(
        increment,
        departure,
        obs_grad,
        obs_weight,
        error_scale,
        corr_blocks,
        corr_pattern.T,
        model_blocks,
        model_pattern.T,
    )
    increment_next = (1.0 - RELAX) * increment + RELAX * x_new.astype(F32)[None]
    dual_next = (1.0 - RELAX) * dual_field + RELAX * d_new.astype(F32)[None]
    return increment_next, dual_next


def solution(mesh):
    field = P("win", "col", None)
    return jax.shard_map(
        body,
        mesh=mesh,
        in_specs=(
            field,
            field,
            field,
            field,
            field,
            P("win", None),
            P("col", None, None),
            P("col", None),
            P("col", None, None),
            P("col", None),
        ),
        out_specs=(field, field),
        check_vma=False,
    )
```

```python
import functools

import jax
import jax.numpy as jnp
from jax import lax
from jax.experimental import pallas as pl
from jax.experimental.pallas import tpu as pltpu
from jax.sharding import PartitionSpec as P

WIN = 8
LEV = 128
SLAB = LEV // WIN
OWN = 1024
BLK = 64
ROWS = OWN // BLK
RU, NNZ_U = 4, 8
RM, NNZ_M = 2, 4
TURN = RM * BLK
HALO = (WIN - 1) * TURN
EXT = OWN + 2 * HALO
END = HALO + OWN
RIM = RU * BLK
M_SIDE = HALO // BLK
M_PAIRS = EXT // 128
FOURS = OWN // 256
EDGES = (-1, 0, FOURS - 1, FOURS)
EARLY = 4
HELD = (5, 3)
G_GROUPS = ((6, 7), (3, 4, 5), (1, 2))
T_GROUPS = ((0, 1), (2, 3), (4, 5, 6))
RELAX = 0.75
MESH = pl.DeviceIdType.MESH
F32 = jnp.float32
BF16 = jnp.bfloat16


def rows_of(window):
    if isinstance(window, int):
        return pl.ds(window * SLAB, SLAB)
    return pl.ds(pl.multiple_of(window * SLAB, SLAB), SLAB)


def lane_index():
    return lax.broadcasted_iota(jnp.int32, (1, 128), 1)


def spread_positions(pattern, first_row, reach, total):
    count = pattern.shape[0]
    own_row = first_row + lax.broadcasted_iota(jnp.int32, (count, ROWS), 1)
    offset = pattern - own_row + reach
    offset = jnp.where(offset < 0, offset + total, offset)
    offset = jnp.where(offset >= total, offset - total, offset)
    offset = jnp.transpose(offset.astype(F32))
    low = lax.broadcasted_iota(jnp.int32, (ROWS, 128), 1) < BLK
    spread = []
    for pair in range(count // 2):
        even = jnp.broadcast_to(offset[:, 2 * pair : 2 * pair + 1], (ROWS, 128))
        odd = jnp.broadcast_to(offset[:, 2 * pair + 1 : 2 * pair + 2], (ROWS, 128))
        spread.append(jnp.where(low, even, odd))
        spread.append(jnp.where(low, odd, even))
    return spread


def place_row(raw, positions, count, first_position):
    terms = []
    for pair in range(raw.shape[1] // 128):
        part = raw[:, pair * 128 : (pair + 1) * 128]
        turned = pltpu.roll(part.astype(F32), BLK, 1).astype(BF16)
        terms.append((part, positions[2 * pair]))
        terms.append((turned, positions[2 * pair + 1]))
    upper = (lane_index() >= BLK).astype(jnp.int32)
    tiles = []
    for v in range(count):
        wanted = (first_position + 2 * v + upper).astype(F32)
        total = None
        for part, position in terms:
            mask = jnp.broadcast_to((position == wanted).astype(F32), (16, 128)).astype(BF16)
            term = part * jnp.concatenate([mask] * (BLK // 16), axis=0)
            total = term if total is None else total + term
        tiles.append(total)
    return tiles


def weights(band, m):
    return jnp.concatenate(
        [band[m - 1 + s, :, 384 - 128 * s : 640 - 128 * s] for s in range(4)], axis=0
    )


def split(value):
    high = value.astype(BF16)
    return high, (value - high.astype(F32)).astype(BF16)


def kernel(
    ncol,
    inc,
    dep,
    og,
    ow,
    es,
    cb,
    cp,
    mb,
    mp,
    x_out,
    d_out,
    inc_v,
    og_v,
    ow_v,
    dep_v,
    es_v,
    g_t,
    dep_t,
    es_t,
    g_f,
    dep_f,
    es_all,
    es_f,
    d_f,
    d_lo,
    s_f,
    p_out,
    p_in,
    p_own,
    i_f,
    t_own,
    t_f,
    x_f,
    x_lo,
    x_r,
    d_r,
    m_raw,
    c_raw,
    m_pat,
    c_pat,
    m_pos,
    c_pos,
    m_band,
    m_turn,
    u_band,
    local_sem,
    g_send,
    g_recv,
    es_send,
    es_recv,
    dep_send,
    dep_recv,
    dr_send,
    dr_recv,
    xr_send,
    xr_recv,
    side_send,
    side_recv,
    gh_send,
    gh_recv,
    p_send,
    p_recv,
    th_send,
    th_recv,
):
    me = lax.axis_index("win")
    col = lax.axis_index("col")
    left = lax.rem(col + ncol - 1, ncol)
    right = lax.rem(col + 1, ncol)
    sides = (left, right)
    partner = me + 1 - 2 * lax.rem(me, 2)
    total_blocks = ncol * ROWS
    own_cols = pl.ds(HALO, OWN)
    whole = pl.ds(0, OWN)
    sent, due = [], {}

    def to_window(src, dst, send, recv, window):
        return pltpu.make_async_remote_copy(
            src_ref=src, dst_ref=dst, send_sem=send, recv_sem=recv,
            device_id=(window, col), device_id_type=MESH,
        )

    def to_side(src, dst, send, recv, side, window=me):
        return pltpu.make_async_remote_copy(
            src_ref=src, dst_ref=dst, send_sem=send, recv_sem=recv,
            device_id=(window, sides[side]), device_id_type=MESH,
        )

    def arrive(*key):
        due.pop(key)()

    def start_sides(key, copies):
        for copy in copies:
            copy.start()
            sent.append(copy.wait_send)
        due[key] = lambda: [copy.wait_recv() for copy in copies]

    def give_out(name, src, dst, cols, sends, recvs):
        for d in (3, 5, 1, 7, 4, 2, 6):
            window = lax.rem(me + d, WIN)
            to_window(
                src.at[rows_of(window), :], dst.at[rows_of(me), cols], sends.at[window], recvs.at[me], window
            ).start()
        for k in range(WIN):
            def slab(k=k):
                return to_window(
                    src.at[rows_of(k), :], dst.at[rows_of(k), cols], sends.at[k], recvs.at[k], k
                )

            def sent_slab(slab=slab, k=k):
                @pl.when(me != k)
                def _():
                    slab().wait_send()

            def due_slab(slab=slab, k=k):
                @pl.when(me != k)
                def _():
                    slab().wait_recv()

            sent.append(sent_slab)
            due[name, k] = due_slab

    def give_back(name, src, dst, k, sends, recvs):
        def back():
            return to_window(src.at[rows_of(k), own_cols], dst.at[rows_of(me), :], sends.at[k], recvs.at[me], k)

        @pl.when(me != k)
        def _():
            back().start()

        @pl.when(me == k)
        def _():
            dst[rows_of(me), :] = src[rows_of(k), HALO:END]

        def sent_back():
            @pl.when(me != k)
            def _():
                back().wait_send()

        sent.append(sent_back)

    def due_back(name, dst, sends, recvs, here):
        def back(k):
            @pl.when((me != k) & here)
            def _():
                to_window(dst.at[rows_of(k), :], dst.at[rows_of(k), :], sends.at[k], recvs.at[k], k).wait_recv()

        for k in range(WIN):
            due[name, k] = lambda k=k: back(k)

    def halo_copies(src, windows, width, sends, recvs):
        window = windows[0]
        rows = pl.ds(window * SLAB, len(windows) * SLAB)
        return (
            to_side(
                src.at[rows, pl.ds(HALO, width)], src.at[rows, pl.ds(END, width)],
                sends.at[window, 0], recvs.at[window, 0], 0,
            ),
            to_side(
                src.at[rows, pl.ds(END - width, width)], src.at[rows, pl.ds(HALO - width, width)],
                sends.at[window, 1], recvs.at[window, 1], 1,
            ),
        )

    def close():
        for key in list(due):
            arrive(*key)
        for wait in sent:
            wait()

    barrier = pltpu.get_barrier_semaphore()
    for d in range(1, WIN):
        pl.semaphore_signal(barrier, inc=1, device_id=(lax.rem(me + d, WIN), col), device_id_type=MESH)
    for window in (me, partner):
        for side in range(2):
            pl.semaphore_signal(barrier, inc=1, device_id=(window, sides[side]), device_id_type=MESH)

    loads = [
        pltpu.make_async_copy(inc.at[0], inc_v, local_sem.at[0]),
        pltpu.make_async_copy(og.at[0], og_v, local_sem.at[1]),
        pltpu.make_async_copy(ow.at[0], ow_v, local_sem.at[2]),
        pltpu.make_async_copy(es, es_v, local_sem.at[3]),
        pltpu.make_async_copy(mp, m_pat.at[1], local_sem.at[4]),
        pltpu.make_async_copy(cp, c_pat, local_sem.at[5]),
        pltpu.make_async_copy(mb, m_raw.at[pl.ds(ROWS, ROWS)], local_sem.at[6]),
        pltpu.make_async_copy(cb, c_raw, local_sem.at[7]),
        pltpu.make_async_copy(dep.at[0], dep_v, local_sem.at[8]),
    ]
    for load in loads:
        load.start()
    for load in loads[:4]:
        load.wait()
    for c in range(OWN // 128):
        at = slice(c * 128, (c + 1) * 128)
        g = ow_v[at, :].astype(F32) * inc_v[at, :] - og_v[at, :]
        g_t[:, at] = jnp.transpose(g).astype(BF16)

    pl.semaphore_wait(barrier, WIN - 1 + 4)

    give_out("g", g_t, g_f, own_cols, g_send, g_recv)
    start_sides(
        ("pattern",),
        (
            to_side(mp, m_pat.at[2], side_send.at[0, 0], side_recv.at[0, 0], 0),
            to_side(mp, m_pat.at[0], side_send.at[0, 1], side_recv.at[0, 1], 1),
        ),
    )
    half = M_SIDE // 2
    across = (lax.rem(col, ncol // 2) == 0, lax.rem(col + 1, ncol // 2) == 0)
    for part in range(2):
        copies = []
        for side, first in ((0, part * half), (1, ROWS - M_SIDE + part * half)):
            rows = (pl.ds(2 * ROWS + first, half), pl.ds(first, half))[side]
            window = jnp.where(across[side], partner, me) if part else me
            copies.append(
                to_side(
                    mb.at[pl.ds(first, half)], m_raw.at[rows],
                    side_send.at[1 + part, side], side_recv.at[1 + part, side], side, window,
                )
            )
        start_sides(("blocks", part), tuple(copies))
    for d in range(1, WIN):
        window = lax.rem(me + d, WIN)
        to_window(es_v, es_all.at[me], es_send.at[window], es_recv.at[me], window).start()
    for k in range(WIN):
        def scale_row(k=k):
            return to_window(es_v, es_all.at[k], es_send.at[k], es_recv.at[k], k)

        def sent_row(row=scale_row, k=k):
            @pl.when(me != k)
            def _():
                row().wait_send()

        def due_row(row=scale_row, k=k):
            @pl.when(me != k)
            def _():
                row().wait_recv()

        sent.append(sent_row)
        due["es", k] = due_row
    es_all[me] = es_v[...]
    g_f[rows_of(me), HALO:END] = g_t[rows_of(me), :]

    loads[8].wait()
    for c in range(OWN // 128):
        at = slice(c * 128, (c + 1) * 128)
        dep_t[:, at] = jnp.transpose(dep_v[at, :]).astype(BF16)

    def store_positions(side):
        where = slice(side * ROWS, (side + 1) * ROWS)
        block = (left, col, right)[side] * ROWS
        for n, value in enumerate(spread_positions(m_pat[side], block, RM, total_blocks)):
            m_pos[n, where, :] = value

    def build_m(first, last):
        def pair(q, carry):
            zero = jnp.zeros((128, 128), BF16)
            m_band[q, :, 0:128] = zero
            m_band[q, :, 512:640] = zero
            for half in range(2):
                row = 2 * q + (ROWS - M_SIDE) + half
                positions = [m_pos[n, pl.ds(row, 1), :] for n in range(NNZ_M)]
                tiles = place_row(m_raw[row], positions, 3, -half)
                for v, tile in enumerate(tiles):
                    m_band[q, half * BLK : (half + 1) * BLK, (v + 1) * 128 : (v + 2) * 128] = tile
            return carry

        lax.fori_loop(first, last, pair, 0)

    def build_u():
        def four(r, carry):
            zero = jnp.zeros((BLK, 128), BF16)
            for sub in range(4):
                row = 4 * r + sub
                where = slice(sub * BLK, (sub + 1) * BLK)
                positions = [c_pos[n, pl.ds(row, 1), :] for n in range(NNZ_U)]
                start = sub // 2
                tiles = place_row(c_raw[row], positions, 5, 2 * start - sub)
                for v, tile in enumerate(tiles):
                    u_band[r, where, (v + start) * 128 : (v + start + 1) * 128] = tile
                u_band[r, where, 5 * (1 - start) * 128 : (5 * (1 - start) + 1) * 128] = zero
            return carry

        lax.fori_loop(0, FOURS, four, 0)

    def turn_tile(p, q_shift):
        tile = m_band[p + q_shift, :, 256 - 128 * q_shift : 384 - 128 * q_shift]
        at = 256 + 128 * q_shift
        m_turn[p, :, at : at + 128] = jnp.transpose(tile)

    def build_turn():
        zero = jnp.zeros((128, 128), BF16)

        def one(p, carry):
            m_turn[p, :, 0:128] = zero
            m_turn[p, :, 512:640] = zero
            for q_shift in (-1, 0, 1):
                turn_tile(p, q_shift)
            return carry

        lax.fori_loop(1, M_PAIRS - 1, one, 0)
        for p, shifts in ((0, (0, 1)), (M_PAIRS - 1, (-1, 0))):
            for v in range(5):
                m_turn[p, :, v * 128 : (v + 1) * 128] = zero
            for q_shift in shifts:
                turn_tile(p, q_shift)

    for load in loads[4:8]:
        load.wait()
    store_positions(1)
    for n, value in enumerate(spread_positions(c_pat[...], col * ROWS, RU, total_blocks)):
        c_pos[n] = value
    side_pairs = M_SIDE // 2
    build_m(side_pairs, side_pairs + ROWS // 2)
    build_u()
    for k in range(WIN - 1, -1, -1):
        arrive("g", k)
        for windows in G_GROUPS:
            if k == windows[0]:
                start_sides(("g halo", windows[-1]), halo_copies(g_f, windows, TURN * windows[-1], gh_send, gh_recv))
    for k in range(WIN):
        arrive("es", k)
    rows = jnp.concatenate([es_all[k] for k in range(WIN)] + [jnp.zeros((128 - WIN, LEV), F32)], axis=0)
    es_t[...] = jnp.transpose(rows)
    columns = es_t[rows_of(me), :]
    for k in range(WIN):
        es_f[rows_of(k), :] = jnp.broadcast_to(columns[:, k : k + 1], (SLAB, 128))
    arrive("pattern")
    store_positions(0)
    store_positions(2)
    arrive("blocks", 0)
    arrive("blocks", 1)
    build_m(0, side_pairs)
    build_m(side_pairs + ROWS // 2, M_PAIRS)

    give_out("dep", dep_t, dep_f, whole, dep_send, dep_recv)
    dep_f[rows_of(me), :] = dep_t[rows_of(me), :]
    def scaled(k):
        scale = jnp.concatenate([es_f[rows_of(k), :]] * 2, axis=1)
        return lambda value: (scale * value).astype(BF16)

    def transposed(rows, c):
        total = None
        for r in range(max(c - 1, 0), min(c + 2, FOURS)):
            at = (c - r + 1) * 256
            term = jnp.dot(
                s_f[rows, r * 256 : (r + 1) * 256], u_band[r, :, at : at + 256], preferred_element_type=F32
            )
            total = term if total is None else total + term
        return total

    def send_rims(part, rows):
        copies = tuple(
            to_side(p_out.at[side, rows, :], p_in.at[1 - side, rows, :], p_send.at[part, side], p_recv.at[part, side], side)
            for side in range(2)
        )
        for side in range(2):
            for n in range(2):
                p_out[side, rows, n * 256 : (n + 1) * 256] = transposed(rows, EDGES[2 * side + n]).astype(BF16)
            copies[side].start()
            sent.append(copies[side].wait_send)
        due["rims", part] = lambda: [copy.wait_recv() for copy in copies]

    last = WIN - 1
    arrive("g halo", last)
    d_f[rows_of(last), :] = g_f[rows_of(last), :]
    scale = scaled(last)
    for r in range(FOURS):
        s_f[rows_of(last), r * 256 : (r + 1) * 256] = scale(
            g_f[rows_of(last), HALO + r * 256 : HALO + (r + 1) * 256].astype(F32)
        )
    for k in range(last - 1, -1, -1):
        if ("g halo", k) in due:
            arrive("g halo", k)
        scale = jnp.concatenate([es_f[rows_of(k), :]] * 2, axis=1)
        for group in range(OWN // 256 + k):
            m = M_SIDE // 2 - k + 2 * group
            at = slice(m * 128, (m + 2) * 128)
            near = slice((m - 1) * 128, (m + 3) * 128)
            field = d_f[rows_of(k + 1), near]
            if k + 1 < last:
                field = jnp.concatenate([field, d_lo[rows_of(k + 1), near]], axis=0)
            product = jnp.dot(field, weights(m_band, m), preferred_element_type=F32)
            if k + 1 < last:
                product = product[:SLAB] + product[SLAB:]
            value = g_f[rows_of(k), at].astype(F32) + product
            d_f[rows_of(k), at], d_lo[rows_of(k), at] = split(value)
            value = (scale * value).astype(BF16)
            for n in range(2):
                c = m + n - M_SIDE // 2
                if 0 <= c < OWN // 128:
                    s_f[rows_of(k), c * 128 : (c + 1) * 128] = value[:, n * 128 : (n + 1) * 128]
        if k == EARLY:
            send_rims(0, slice(EARLY * SLAB, LEV))
    send_rims(1, slice(0, EARLY * SLAB))

    every_row = slice(0, LEV)
    for c in range(1, FOURS - 1):
        i_f[:, (c + 1) * 256 : (c + 2) * 256] = transposed(every_row, c).astype(BF16)
    for n, c in enumerate(EDGES):
        p_own[:, n * 256 : (n + 1) * 256] = transposed(every_row, c)
    build_turn()
    for k in range(WIN):
        arrive("dep", k)
    arrive("rims", 0)
    arrive("rims", 1)
    for n, c in enumerate(EDGES):
        there = p_in[n // 2, :, (n % 2) * 256 : (n % 2 + 1) * 256].astype(F32)
        i_f[:, (c + 1) * 256 : (c + 2) * 256] = (p_own[:, n * 256 : (n + 1) * 256] + there).astype(BF16)
    scale = es_f[...]
    scale = jnp.concatenate([scale, scale], axis=1)
    for r in range(FOURS):
        product = lax.dot_general(
            i_f[:, r * 256 : r * 256 + 768], u_band[r], (((1,), (1,)), ((), ())), preferred_element_type=F32
        )
        at = slice(r * 256, (r + 1) * 256)
        value = dep_f[:, at].astype(F32) - scale * product
        t_own[:, at] = value
        t_f[:, HALO + r * 256 : HALO + (r + 1) * 256] = value.astype(BF16)
    for k in range(last):
        give_back("d", d_f, d_r, k, dr_send, dr_recv)
    due_back("d", d_r, dr_send, dr_recv, me != last)

    for windows in T_GROUPS:
        start_sides(
            ("t halo", windows[0]), halo_copies(t_f, windows, HALO - TURN * windows[0], th_send, th_recv)
        )

    def target(k, m):
        c = m - M_SIDE // 2
        if 0 <= c < OWN // 128:
            return t_own[rows_of(k), c * 128 : (c + 1) * 128]
        return t_f[rows_of(k), m * 128 : (m + 1) * 128].astype(F32)

    for c in range(OWN // 128):
        at = slice(HALO + c * 128, HALO + (c + 1) * 128)
        x_f[rows_of(0), at], x_lo[rows_of(0), at] = split(t_own[rows_of(0), c * 128 : (c + 1) * 128])
    give_back("x", x_f, x_r, 0, xr_send, xr_recv)
    arrive("t halo", 0)
    for at in (slice(0, HALO), slice(END, EXT)):
        x_f[rows_of(0), at] = t_f[rows_of(0), at]
        x_lo[rows_of(0), at] = jnp.zeros((SLAB, HALO), BF16)
    for k in range(1, WIN):
        if ("t halo", k) in due:
            arrive("t halo", k)
        for group in range(OWN // 256 + WIN - 1 - k):
            m = k + 2 * group
            at = slice(m * 128, (m + 2) * 128)
            near = slice((m - 1) * 128, (m + 3) * 128)
            field = jnp.concatenate([x_f[rows_of(k - 1), near], x_lo[rows_of(k - 1), near]], axis=0)
            product = jnp.dot(field, weights(m_turn, m), preferred_element_type=F32)
            base = jnp.concatenate([target(k, m), target(k, m + 1)], axis=1)
            x_f[rows_of(k), at], x_lo[rows_of(k), at] = split(base + product[:SLAB] + product[SLAB:])
        if k not in HELD:
            give_back("x", x_f, x_r, k, xr_send, xr_recv)
    for k in HELD:
        give_back("x", x_f, x_r, k, xr_send, xr_recv)
    due_back("x", x_r, xr_send, xr_recv, me >= 0)

    def finish(name, result, out):
        for k in range(WIN):
            arrive(name, k)
        for c in range(OWN // 128):
            at = slice(c * 128, (c + 1) * 128)
            out[at, :] = jnp.transpose(result[:, at].astype(F32)).astype(BF16)

    @pl.when(me == last)
    def _():
        d_r[...] = g_t[...]

    finish("d", d_r, d_out)
    for wait in sent:
        wait()
    sent.clear()
    finish("x", x_r, x_out)
    close()


def body(
    increment,
    dual_field,
    departure,
    obs_grad,
    obs_weight,
    error_scale,
    corr_blocks,
    corr_pattern,
    model_blocks,
    model_pattern,
):
    ncol = lax.axis_size("col")
    vmem = pltpu.VMEM
    dma = pltpu.SemaphoreType.DMA
    hbm = pl.BlockSpec(memory_space=pltpu.HBM)
    x_new, d_new = pl.pallas_call(
        functools.partial(kernel, ncol),
        out_shape=[pltpu.VMEM((OWN, LEV), BF16)] * 2,
        in_specs=[hbm] * 9,
        out_specs=[pl.BlockSpec(memory_space=pltpu.VMEM)] * 2,
        scratch_shapes=[
            vmem((OWN, LEV), F32),
            vmem((OWN, LEV), F32),
            vmem((OWN, LEV), BF16),
            vmem((OWN, LEV), F32),
            vmem((1, LEV), F32),
            vmem((LEV, OWN), BF16),
            vmem((LEV, OWN), BF16),
            vmem((LEV, 128), F32),
            vmem((LEV, EXT), BF16),
            vmem((LEV, OWN), BF16),
            vmem((WIN, 1, LEV), F32),
            vmem((LEV, 128), F32),
            vmem((LEV, EXT), BF16),
            vmem((LEV, EXT), BF16),
            vmem((LEV, OWN), BF16),
            vmem((2, LEV, 2 * RIM), BF16),
            vmem((2, LEV, 2 * RIM), BF16),
            vmem((LEV, 4 * RIM), F32),
            vmem((LEV, OWN + 2 * RIM), BF16),
            vmem((LEV, OWN), F32),
            vmem((LEV, EXT), BF16),
            vmem((LEV, EXT), BF16),
            vmem((LEV, EXT), BF16),
            vmem((LEV, OWN), BF16),
            vmem((LEV, OWN), BF16),
            vmem((3 * ROWS, BLK, NNZ_M * BLK), BF16),
            vmem((ROWS, BLK, NNZ_U * BLK), BF16),
            vmem((3, NNZ_M, ROWS), jnp.int32),
            vmem((NNZ_U, ROWS), jnp.int32),
            vmem((NNZ_M, 3 * ROWS, 128), F32),
            vmem((NNZ_U, ROWS, 128), F32),
            vmem((M_PAIRS, 128, 640), BF16),
            vmem((M_PAIRS, 128, 640), BF16),
            vmem((FOURS, 256, 768), BF16),
            dma((9,)),
        ]
        + [dma((WIN,))] * 10
        + [dma((3, 2))] * 2
        + [dma((WIN, 2))] * 2
        + [dma((2, 2))] * 2
        + [dma((WIN, 2))] * 2,
        compiler_params=pltpu.CompilerParams(
            collective_id=0, has_side_effects=True, vmem_limit_bytes=56 * 1024 * 1024
        ),
    )(
        increment,
        departure,
        obs_grad,
        obs_weight,
        error_scale,
        corr_blocks,
        corr_pattern.T,
        model_blocks,
        model_pattern.T,
    )
    increment_next = (1.0 - RELAX) * increment + RELAX * x_new.astype(F32)[None]
    dual_next = (1.0 - RELAX) * dual_field + RELAX * d_new.astype(F32)[None]
    return increment_next, dual_next


def solution(mesh):
    field = P("win", "col", None)
    return jax.shard_map(
        body,
        mesh=mesh,
        in_specs=(
            field,
            field,
            field,
            field,
            field,
            P("win", None),
            P("col", None, None),
            P("col", None),
            P("col", None, None),
            P("col", None),
        ),
        out_specs=(field, field),
        check_vma=False,
    )
```

```python
import functools

import jax
import jax.numpy as jnp
from jax import lax
from jax.experimental import pallas as pl
from jax.experimental.pallas import tpu as pltpu
from jax.sharding import PartitionSpec as P

WIN = 8
LEV = 128
SLAB = LEV // WIN
OWN = 1024
BLK = 64
ROWS = OWN // BLK
RU, NNZ_U = 4, 8
RM, NNZ_M = 2, 4
TURN = RM * BLK
ALONE = 3
HALO = (WIN - 1 - ALONE) * TURN
EXT = OWN + 2 * HALO
END = HALO + OWN
RIM = RU * BLK
M_SIDE = HALO // BLK
M_PAIRS = EXT // 128
FOURS = OWN // 256
EDGES = (-1, 0, FOURS - 1, FOURS)
EARLY = 4
HELD = (5, 3)
SIDE = HALO // 128
TILES = OWN // 128
G_GROUPS = (((5, 6, 7), 256), ((3, 4), 384), ((1, 2), 256))
T_GROUPS = (((0, 1, 2), 256), ((3, 4), 384), ((5, 6), 256))
RELAX = 0.75
MESH = pl.DeviceIdType.MESH
F32 = jnp.float32
BF16 = jnp.bfloat16


def rows_of(window):
    if isinstance(window, int):
        return pl.ds(window * SLAB, SLAB)
    return pl.ds(pl.multiple_of(window * SLAB, SLAB), SLAB)


def lane_index():
    return lax.broadcasted_iota(jnp.int32, (1, 128), 1)


def spread_positions(pattern, first_row, reach, total):
    count = pattern.shape[0]
    own_row = first_row + lax.broadcasted_iota(jnp.int32, (count, ROWS), 1)
    offset = pattern - own_row + reach
    offset = jnp.where(offset < 0, offset + total, offset)
    offset = jnp.where(offset >= total, offset - total, offset)
    offset = jnp.transpose(offset.astype(F32))
    low = lax.broadcasted_iota(jnp.int32, (ROWS, 128), 1) < BLK
    spread = []
    for pair in range(count // 2):
        even = jnp.broadcast_to(offset[:, 2 * pair : 2 * pair + 1], (ROWS, 128))
        odd = jnp.broadcast_to(offset[:, 2 * pair + 1 : 2 * pair + 2], (ROWS, 128))
        spread.append(jnp.where(low, even, odd))
        spread.append(jnp.where(low, odd, even))
    return spread


def place_row(raw, positions, count, first_position):
    terms = []
    for pair in range(raw.shape[1] // 128):
        part = raw[:, pair * 128 : (pair + 1) * 128]
        turned = pltpu.roll(part.astype(F32), BLK, 1).astype(BF16)
        terms.append((part, positions[2 * pair]))
        terms.append((turned, positions[2 * pair + 1]))
    upper = (lane_index() >= BLK).astype(jnp.int32)
    tiles = []
    for v in range(count):
        wanted = (first_position + 2 * v + upper).astype(F32)
        total = None
        for part, position in terms:
            mask = jnp.broadcast_to((position == wanted).astype(F32), (16, 128)).astype(BF16)
            term = part * jnp.concatenate([mask] * (BLK // 16), axis=0)
            total = term if total is None else total + term
        tiles.append(total)
    return tiles


def weights(band, m):
    return jnp.concatenate(
        [band[m - 1 + s, :, 384 - 128 * s : 640 - 128 * s] for s in range(4)], axis=0
    )


def split(value):
    high = value.astype(BF16)
    return high, (value - high.astype(F32)).astype(BF16)


def kernel(
    ncol,
    inc,
    dep,
    og,
    ow,
    es,
    cb,
    cp,
    mb,
    mp,
    x_out,
    d_out,
    inc_v,
    og_v,
    ow_v,
    dep_v,
    es_v,
    g_t,
    dep_t,
    es_t,
    g_f,
    dep_f,
    es_all,
    es_f,
    d_f,
    d_lo,
    s_f,
    p_out,
    p_in,
    p_own,
    i_f,
    t_own,
    t_f,
    x_f,
    x_lo,
    x_r,
    d_r,
    m_raw,
    c_raw,
    m_pat,
    c_pat,
    m_pos,
    c_pos,
    m_band,
    m_turn,
    u_band,
    local_sem,
    g_send,
    g_recv,
    es_send,
    es_recv,
    dep_send,
    dep_recv,
    dr_send,
    dr_recv,
    xr_send,
    xr_recv,
    side_send,
    side_recv,
    gh_send,
    gh_recv,
    dh_send,
    dh_recv,
    xh_send,
    xh_recv,
    p_send,
    p_recv,
    th_send,
    th_recv,
):
    me = lax.axis_index("win")
    col = lax.axis_index("col")
    left = lax.rem(col + ncol - 1, ncol)
    right = lax.rem(col + 1, ncol)
    sides = (left, right)
    partner = me + 1 - 2 * lax.rem(me, 2)
    total_blocks = ncol * ROWS
    own_cols = pl.ds(HALO, OWN)
    whole = pl.ds(0, OWN)
    sent, due = [], {}

    def to_window(src, dst, send, recv, window):
        return pltpu.make_async_remote_copy(
            src_ref=src, dst_ref=dst, send_sem=send, recv_sem=recv,
            device_id=(window, col), device_id_type=MESH,
        )

    def to_side(src, dst, send, recv, side, window=me):
        return pltpu.make_async_remote_copy(
            src_ref=src, dst_ref=dst, send_sem=send, recv_sem=recv,
            device_id=(window, sides[side]), device_id_type=MESH,
        )

    def arrive(*key):
        due.pop(key)()

    def start_sides(key, copies):
        for copy in copies:
            copy.start()
            sent.append(copy.wait_send)
        due[key] = lambda: [copy.wait_recv() for copy in copies]

    def give_out(name, src, dst, cols, sends, recvs):
        for d in (3, 5, 1, 7, 4, 2, 6):
            window = lax.rem(me + d, WIN)
            to_window(
                src.at[rows_of(window), :], dst.at[rows_of(me), cols], sends.at[window], recvs.at[me], window
            ).start()
        for k in range(WIN):
            def slab(k=k):
                return to_window(
                    src.at[rows_of(k), :], dst.at[rows_of(k), cols], sends.at[k], recvs.at[k], k
                )

            def sent_slab(slab=slab, k=k):
                @pl.when(me != k)
                def _():
                    slab().wait_send()

            def due_slab(slab=slab, k=k):
                @pl.when(me != k)
                def _():
                    slab().wait_recv()

            sent.append(sent_slab)
            due[name, k] = due_slab

    def give_back(name, src, dst, k, sends, recvs):
        def back():
            return to_window(src.at[rows_of(k), own_cols], dst.at[rows_of(me), :], sends.at[k], recvs.at[me], k)

        @pl.when(me != k)
        def _():
            back().start()

        @pl.when(me == k)
        def _():
            dst[rows_of(me), :] = src[rows_of(k), HALO:END]

        def sent_back():
            @pl.when(me != k)
            def _():
                back().wait_send()

        sent.append(sent_back)

    def due_back(name, dst, sends, recvs, here):
        def back(k):
            @pl.when((me != k) & here)
            def _():
                to_window(dst.at[rows_of(k), :], dst.at[rows_of(k), :], sends.at[k], recvs.at[k], k).wait_recv()

        for k in range(WIN):
            due[name, k] = lambda k=k: back(k)

    def halo_copies(src, windows, first, end, sends, recvs):
        window = windows[0]
        rows = pl.ds(window * SLAB, len(windows) * SLAB)
        n = end - first
        return (
            to_side(
                src.at[rows, pl.ds(HALO + first, n)], src.at[rows, pl.ds(END + first, n)],
                sends.at[window, 0], recvs.at[window, 0], 0,
            ),
            to_side(
                src.at[rows, pl.ds(END - end, n)], src.at[rows, pl.ds(HALO - end, n)],
                sends.at[window, 1], recvs.at[window, 1], 1,
            ),
        )

    def turn_halo(name, src, window, turn, sends, recvs):
        start_sides((name, window), halo_copies(src, (window,), TURN * turn, min(TURN * (turn + 2), HALO), sends, recvs))

    def alone(turn):
        return [SIDE + turn + 2 * group for group in range(TILES // 2 - turn)]

    def rims_of(turn):
        return [first + 2 * group for first in (SIDE - turn, SIDE + TILES - turn) for group in range(turn)]

    def wide(reach):
        return [SIDE - reach + 2 * group for group in range(TILES // 2 + reach)]

    def close():
        for key in list(due):
            arrive(*key)
        for wait in sent:
            wait()

    barrier = pltpu.get_barrier_semaphore()
    for d in range(1, WIN):
        pl.semaphore_signal(barrier, inc=1, device_id=(lax.rem(me + d, WIN), col), device_id_type=MESH)
    for window in (me, partner):
        for side in range(2):
            pl.semaphore_signal(barrier, inc=1, device_id=(window, sides[side]), device_id_type=MESH)

    loads = [
        pltpu.make_async_copy(inc.at[0], inc_v, local_sem.at[0]),
        pltpu.make_async_copy(og.at[0], og_v, local_sem.at[1]),
        pltpu.make_async_copy(ow.at[0], ow_v, local_sem.at[2]),
        pltpu.make_async_copy(es, es_v, local_sem.at[3]),
        pltpu.make_async_copy(mp, m_pat.at[1], local_sem.at[4]),
        pltpu.make_async_copy(cp, c_pat, local_sem.at[5]),
        pltpu.make_async_copy(mb, m_raw.at[pl.ds(ROWS, ROWS)], local_sem.at[6]),
        pltpu.make_async_copy(cb, c_raw, local_sem.at[7]),
        pltpu.make_async_copy(dep.at[0], dep_v, local_sem.at[8]),
    ]
    for load in loads:
        load.start()
    for load in loads[:4]:
        load.wait()
    for c in range(OWN // 128):
        at = slice(c * 128, (c + 1) * 128)
        g = ow_v[at, :].astype(F32) * inc_v[at, :] - og_v[at, :]
        g_t[:, at] = jnp.transpose(g).astype(BF16)

    pl.semaphore_wait(barrier, WIN - 1 + 4)

    give_out("g", g_t, g_f, own_cols, g_send, g_recv)
    start_sides(
        ("pattern",),
        (
            to_side(mp, m_pat.at[2], side_send.at[0, 0], side_recv.at[0, 0], 0),
            to_side(mp, m_pat.at[0], side_send.at[0, 1], side_recv.at[0, 1], 1),
        ),
    )
    half = M_SIDE // 2
    across = (lax.rem(col, ncol // 2) == 0, lax.rem(col + 1, ncol // 2) == 0)
    for part in range(2):
        copies = []
        for side, first in ((0, part * half), (1, ROWS - M_SIDE + part * half)):
            rows = (pl.ds(2 * ROWS + first, half), pl.ds(first, half))[side]
            window = jnp.where(across[side], partner, me) if part else me
            copies.append(
                to_side(
                    mb.at[pl.ds(first, half)], m_raw.at[rows],
                    side_send.at[1 + part, side], side_recv.at[1 + part, side], side, window,
                )
            )
        start_sides(("blocks", part), tuple(copies))
    for d in range(1, WIN):
        window = lax.rem(me + d, WIN)
        to_window(es_v, es_all.at[me], es_send.at[window], es_recv.at[me], window).start()
    for k in range(WIN):
        def scale_row(k=k):
            return to_window(es_v, es_all.at[k], es_send.at[k], es_recv.at[k], k)

        def sent_row(row=scale_row, k=k):
            @pl.when(me != k)
            def _():
                row().wait_send()

        def due_row(row=scale_row, k=k):
            @pl.when(me != k)
            def _():
                row().wait_recv()

        sent.append(sent_row)
        due["es", k] = due_row
    es_all[me] = es_v[...]
    g_f[rows_of(me), HALO:END] = g_t[rows_of(me), :]

    loads[8].wait()
    for c in range(OWN // 128):
        at = slice(c * 128, (c + 1) * 128)
        dep_t[:, at] = jnp.transpose(dep_v[at, :]).astype(BF16)

    def store_positions(side):
        where = slice(side * ROWS, (side + 1) * ROWS)
        block = (left, col, right)[side] * ROWS
        for n, value in enumerate(spread_positions(m_pat[side], block, RM, total_blocks)):
            m_pos[n, where, :] = value

    def build_m(first, last):
        def pair(q, carry):
            zero = jnp.zeros((128, 128), BF16)
            m_band[q, :, 0:128] = zero
            m_band[q, :, 512:640] = zero
            for half in range(2):
                row = 2 * q + (ROWS - M_SIDE) + half
                positions = [m_pos[n, pl.ds(row, 1), :] for n in range(NNZ_M)]
                tiles = place_row(m_raw[row], positions, 3, -half)
                for v, tile in enumerate(tiles):
                    m_band[q, half * BLK : (half + 1) * BLK, (v + 1) * 128 : (v + 2) * 128] = tile
            return carry

        lax.fori_loop(first, last, pair, 0)

    def build_u():
        def four(r, carry):
            zero = jnp.zeros((BLK, 128), BF16)
            for sub in range(4):
                row = 4 * r + sub
                where = slice(sub * BLK, (sub + 1) * BLK)
                positions = [c_pos[n, pl.ds(row, 1), :] for n in range(NNZ_U)]
                start = sub // 2
                tiles = place_row(c_raw[row], positions, 5, 2 * start - sub)
                for v, tile in enumerate(tiles):
                    u_band[r, where, (v + start) * 128 : (v + start + 1) * 128] = tile
                u_band[r, where, 5 * (1 - start) * 128 : (5 * (1 - start) + 1) * 128] = zero
            return carry

        lax.fori_loop(0, FOURS, four, 0)

    def turn_tile(p, q_shift):
        tile = m_band[p + q_shift, :, 256 - 128 * q_shift : 384 - 128 * q_shift]
        at = 256 + 128 * q_shift
        m_turn[p, :, at : at + 128] = jnp.transpose(tile)

    def build_turn():
        zero = jnp.zeros((128, 128), BF16)

        def one(p, carry):
            m_turn[p, :, 0:128] = zero
            m_turn[p, :, 512:640] = zero
            for q_shift in (-1, 0, 1):
                turn_tile(p, q_shift)
            return carry

        lax.fori_loop(1, M_PAIRS - 1, one, 0)
        for p, shifts in ((0, (0, 1)), (M_PAIRS - 1, (-1, 0))):
            for v in range(5):
                m_turn[p, :, v * 128 : (v + 1) * 128] = zero
            for q_shift in shifts:
                turn_tile(p, q_shift)

    for load in loads[4:8]:
        load.wait()
    store_positions(1)
    for n, value in enumerate(spread_positions(c_pat[...], col * ROWS, RU, total_blocks)):
        c_pos[n] = value
    side_pairs = M_SIDE // 2
    build_m(side_pairs, side_pairs + ROWS // 2)
    build_u()
    for k in range(WIN):
        arrive("es", k)
    rows = jnp.concatenate([es_all[k] for k in range(WIN)] + [jnp.zeros((128 - WIN, LEV), F32)], axis=0)
    es_t[...] = jnp.transpose(rows)
    columns = es_t[rows_of(me), :]
    for k in range(WIN):
        es_f[rows_of(k), :] = jnp.broadcast_to(columns[:, k : k + 1], (SLAB, 128))
    for field in (d_lo, x_lo):
        for first in (0, END):
            field[:, first : first + HALO] = jnp.zeros((LEV, HALO), BF16)
    for k in range(WIN - 1, -1, -1):
        arrive("g", k)
        for windows, width in G_GROUPS:
            if k == windows[0]:
                start_sides(("g halo", windows[0]), halo_copies(g_f, windows, 0, width, gh_send, gh_recv))

    def back(k, m):
        at = slice(m * 128, (m + 2) * 128)
        near = slice((m - 1) * 128, (m + 3) * 128)
        if k + 1 < WIN - 1:
            field = jnp.concatenate([d_f[rows_of(k + 1), near], d_lo[rows_of(k + 1), near]], axis=0)
        else:
            field = g_f[rows_of(k + 1), near]
        product = jnp.dot(field, weights(m_band, m), preferred_element_type=F32)
        if k + 1 < WIN - 1:
            product = product[:SLAB] + product[SLAB:]
        value = g_f[rows_of(k), at].astype(F32) + product
        d_f[rows_of(k), at], d_lo[rows_of(k), at] = split(value)
        value = (jnp.concatenate([es_f[rows_of(k), :]] * 2, axis=1) * value).astype(BF16)
        for n in range(2):
            c = m + n - SIDE
            if 0 <= c < TILES:
                s_f[rows_of(k), c * 128 : (c + 1) * 128] = value[:, n * 128 : (n + 1) * 128]

    last = WIN - 1
    for turn in range(1, ALONE + 1):
        for m in alone(turn):
            back(last - turn, m)
        turn_halo("d halo", d_f, last - turn, turn, dh_send, dh_recv)
    give_out("dep", dep_t, dep_f, whole, dep_send, dep_recv)
    dep_f[rows_of(me), :] = dep_t[rows_of(me), :]
    arrive("pattern")
    store_positions(0)
    store_positions(2)
    arrive("blocks", 0)
    arrive("blocks", 1)
    build_m(0, side_pairs)
    build_m(side_pairs + ROWS // 2, M_PAIRS)

    def scaled(k):
        scale = jnp.concatenate([es_f[rows_of(k), :]] * 2, axis=1)
        return lambda value: (scale * value).astype(BF16)

    def transposed(rows, c):
        total = None
        for r in range(max(c - 1, 0), min(c + 2, FOURS)):
            at = (c - r + 1) * 256
            term = jnp.dot(
                s_f[rows, r * 256 : (r + 1) * 256], u_band[r, :, at : at + 256], preferred_element_type=F32
            )
            total = term if total is None else total + term
        return total

    def send_rims(part, rows):
        copies = tuple(
            to_side(p_out.at[side, rows, :], p_in.at[1 - side, rows, :], p_send.at[part, side], p_recv.at[part, side], side)
            for side in range(2)
        )
        for side in range(2):
            for n in range(2):
                p_out[side, rows, n * 256 : (n + 1) * 256] = transposed(rows, EDGES[2 * side + n]).astype(BF16)
            copies[side].start()
            sent.append(copies[side].wait_send)
        due["rims", part] = lambda: [copy.wait_recv() for copy in copies]

    scale = scaled(last)
    for r in range(FOURS):
        s_f[rows_of(last), r * 256 : (r + 1) * 256] = scale(
            g_f[rows_of(last), HALO + r * 256 : HALO + (r + 1) * 256].astype(F32)
        )
    for windows, _ in G_GROUPS:
        arrive("g halo", windows[0])
    for turn in range(1, WIN):
        k = last - turn
        for m in rims_of(turn) if turn <= ALONE else wide(k):
            back(k, m)
        if turn <= ALONE:
            arrive("d halo", k)
        if k == EARLY:
            send_rims(0, slice(EARLY * SLAB, LEV))
    send_rims(1, slice(0, EARLY * SLAB))
    for k in range(last):
        give_back("d", d_f, d_r, k, dr_send, dr_recv)
    due_back("d", d_r, dr_send, dr_recv, me != last)

    every_row = slice(0, LEV)
    for c in range(1, FOURS - 1):
        i_f[:, (c + 1) * 256 : (c + 2) * 256] = transposed(every_row, c).astype(BF16)
    for n, c in enumerate(EDGES):
        p_own[:, n * 256 : (n + 1) * 256] = transposed(every_row, c)
    build_turn()
    for k in range(WIN):
        arrive("dep", k)
    arrive("rims", 0)
    arrive("rims", 1)
    for n, c in enumerate(EDGES):
        there = p_in[n // 2, :, (n % 2) * 256 : (n % 2 + 1) * 256].astype(F32)
        i_f[:, (c + 1) * 256 : (c + 2) * 256] = (p_own[:, n * 256 : (n + 1) * 256] + there).astype(BF16)
    scale = es_f[...]
    scale = jnp.concatenate([scale, scale], axis=1)
    for r in range(FOURS):
        product = lax.dot_general(
            i_f[:, r * 256 : r * 256 + 768], u_band[r], (((1,), (1,)), ((), ())), preferred_element_type=F32
        )
        at = slice(r * 256, (r + 1) * 256)
        value = dep_f[:, at].astype(F32) - scale * product
        t_own[:, at] = value
        t_f[:, HALO + r * 256 : HALO + (r + 1) * 256] = value.astype(BF16)

    for windows, width in T_GROUPS:
        start_sides(("t halo", windows[0]), halo_copies(t_f, windows, 0, width, th_send, th_recv))

    def target(k, m):
        c = m - SIDE
        if 0 <= c < TILES:
            return t_own[rows_of(k), c * 128 : (c + 1) * 128]
        return t_f[rows_of(k), m * 128 : (m + 1) * 128].astype(F32)

    def fore(k, m):
        at = slice(m * 128, (m + 2) * 128)
        near = slice((m - 1) * 128, (m + 3) * 128)
        field = jnp.concatenate([x_f[rows_of(k - 1), near], x_lo[rows_of(k - 1), near]], axis=0)
        product = jnp.dot(field, weights(m_turn, m), preferred_element_type=F32)
        base = jnp.concatenate([target(k, m), target(k, m + 1)], axis=1)
        x_f[rows_of(k), at], x_lo[rows_of(k), at] = split(base + product[:SLAB] + product[SLAB:])

    for c in range(TILES):
        at = slice(HALO + c * 128, HALO + (c + 1) * 128)
        x_f[rows_of(0), at], x_lo[rows_of(0), at] = split(t_own[rows_of(0), c * 128 : (c + 1) * 128])
    for k in range(1, ALONE + 1):
        for m in alone(k):
            fore(k, m)
        turn_halo("x halo", x_f, k, k, xh_send, xh_recv)
    give_back("x", x_f, x_r, 0, xr_send, xr_recv)
    for windows, _ in T_GROUPS:
        arrive("t halo", windows[0])
    for first in (HALO - 2 * TURN, END):
        at = slice(first, first + 2 * TURN)
        x_f[rows_of(0), at] = t_f[rows_of(0), at]
    for k in range(1, WIN):
        for m in rims_of(k) if k <= ALONE else wide(last - k):
            fore(k, m)
        if k <= ALONE:
            arrive("x halo", k)
        if k not in HELD:
            give_back("x", x_f, x_r, k, xr_send, xr_recv)
    for k in HELD:
        give_back("x", x_f, x_r, k, xr_send, xr_recv)
    due_back("x", x_r, xr_send, xr_recv, me >= 0)

    def finish(name, result, out):
        for k in range(WIN):
            arrive(name, k)
        for c in range(OWN // 128):
            at = slice(c * 128, (c + 1) * 128)
            out[at, :] = jnp.transpose(result[:, at].astype(F32)).astype(BF16)

    @pl.when(me == last)
    def _():
        d_r[...] = g_t[...]

    finish("d", d_r, d_out)
    for wait in sent:
        wait()
    sent.clear()
    finish("x", x_r, x_out)
    close()


def body(
    increment,
    dual_field,
    departure,
    obs_grad,
    obs_weight,
    error_scale,
    corr_blocks,
    corr_pattern,
    model_blocks,
    model_pattern,
):
    ncol = lax.axis_size("col")
    vmem = pltpu.VMEM
    dma = pltpu.SemaphoreType.DMA
    hbm = pl.BlockSpec(memory_space=pltpu.HBM)
    x_new, d_new = pl.pallas_call(
        functools.partial(kernel, ncol),
        out_shape=[pltpu.VMEM((OWN, LEV), BF16)] * 2,
        in_specs=[hbm] * 9,
        out_specs=[pl.BlockSpec(memory_space=pltpu.VMEM)] * 2,
        scratch_shapes=[
            vmem((OWN, LEV), F32),
            vmem((OWN, LEV), F32),
            vmem((OWN, LEV), BF16),
            vmem((OWN, LEV), F32),
            vmem((1, LEV), F32),
            vmem((LEV, OWN), BF16),
            vmem((LEV, OWN), BF16),
            vmem((LEV, 128), F32),
            vmem((LEV, EXT), BF16),
            vmem((LEV, OWN), BF16),
            vmem((WIN, 1, LEV), F32),
            vmem((LEV, 128), F32),
            vmem((LEV, EXT), BF16),
            vmem((LEV, EXT), BF16),
            vmem((LEV, OWN), BF16),
            vmem((2, LEV, 2 * RIM), BF16),
            vmem((2, LEV, 2 * RIM), BF16),
            vmem((LEV, 4 * RIM), F32),
            vmem((LEV, OWN + 2 * RIM), BF16),
            vmem((LEV, OWN), F32),
            vmem((LEV, EXT), BF16),
            vmem((LEV, EXT), BF16),
            vmem((LEV, EXT), BF16),
            vmem((LEV, OWN), BF16),
            vmem((LEV, OWN), BF16),
            vmem((3 * ROWS, BLK, NNZ_M * BLK), BF16),
            vmem((ROWS, BLK, NNZ_U * BLK), BF16),
            vmem((3, NNZ_M, ROWS), jnp.int32),
            vmem((NNZ_U, ROWS), jnp.int32),
            vmem((NNZ_M, 3 * ROWS, 128), F32),
            vmem((NNZ_U, ROWS, 128), F32),
            vmem((M_PAIRS, 128, 640), BF16),
            vmem((M_PAIRS, 128, 640), BF16),
            vmem((FOURS, 256, 768), BF16),
            dma((9,)),
        ]
        + [dma((WIN,))] * 10
        + [dma((3, 2))] * 2
        + [dma((WIN, 2))] * 6
        + [dma((2, 2))] * 2
        + [dma((WIN, 2))] * 2,
        compiler_params=pltpu.CompilerParams(
            collective_id=0, has_side_effects=True, vmem_limit_bytes=56 * 1024 * 1024
        ),
    )(
        increment,
        departure,
        obs_grad,
        obs_weight,
        error_scale,
        corr_blocks,
        corr_pattern.T,
        model_blocks,
        model_pattern.T,
    )
    increment_next = (1.0 - RELAX) * increment + RELAX * x_new.astype(F32)[None]
    dual_next = (1.0 - RELAX) * dual_field + RELAX * d_new.astype(F32)[None]
    return increment_next, dual_next


def solution(mesh):
    field = P("win", "col", None)
    return jax.shard_map(
        body,
        mesh=mesh,
        in_specs=(
            field,
            field,
            field,
            field,
            field,
            P("win", None),
            P("col", None, None),
            P("col", None),
            P("col", None, None),
            P("col", None),
        ),
        out_specs=(field, field),
        check_vma=False,
    )
```
